128 devices in a mesh: dp: 8 (over x, core), mp: 16 (over z, y).
Axes of the slice: x: 4, y: 4, z: 4, core: 2. Of those that a mesh axis runs over, the one named last changes fastest.
Arguments:
- tokens: bfloat16 [16384, 2048], P(('dp', 'mp')), may hold values from -6 to 6
- doc_start: int32 [16384], P('dp'), may hold values from 0 to 1, as said below
- gain_first: float32 [2048], replicated, may hold values from 0.5 to 1.5
- w_query: bfloat16 [2048, 256], P(None, 'mp'), may hold values from -0.125 to 0.125
- w_key: bfloat16 [2048, 256], P(None, 'mp'), may hold values from -0.125 to 0.125
- w_value: bfloat16 [2048, 2048], P(None, 'mp'), may hold values from -0.125 to 0.125
- w_out: bfloat16 [2048, 2048], P('mp'), may hold values from -0.5 to 0.5
- gain_second: float32 [2048], replicated, may hold values from 0.5 to 1.5
- w_gate: bfloat16 [2048, 5632], P(None, 'mp'), may hold values from -0.125 to 0.125
- w_up: bfloat16 [2048, 5632], P(None, 'mp'), may hold values from -0.125 to 0.125
- w_down: bfloat16 [5632, 2048], P('mp'), may hold values from -0.078125 to 0.078125
- out_grad: bfloat16 [16384, 2048], P(('dp', 'mp')), may hold values from -6 to 6
Outputs:
- block_out: float32 [16384, 2048], P(('dp', 'mp'))
- input_grad: float32 [16384, 2048], P(('dp', 'mp'))
- grad_gain_first: float32 [2048], replicated
- grad_query: float32 [2048, 256], P(None, 'mp')
- grad_key: float32 [2048, 256], P(None, 'mp')
- grad_value: float32 [2048, 2048], P(None, 'mp')
- grad_out: float32 [2048, 2048], P('mp')
- grad_gain_second: float32 [2048], replicated
- grad_gate: float32 [2048, 5632], P(None, 'mp')
- grad_up: float32 [2048, 5632], P(None, 'mp')
- grad_down: float32 [5632, 2048], P('mp')
The draws below stay inside these ranges and needn't reach their ends.
Inputs may be any that keep to these rules, and one draw needn't show every extreme that they name: `doc_start`: 1 marks the first token of a document and 0 the others; the first token of every row of 2048 tokens is marked.
All inputs are finite; a program needn't handle non-finite values.
Results may differ from the reference program's by a relative error of at most 0.025.
Values may be sent and summed in bfloat16 or wider, within the bound.
No kernel may reach another device: no remote copies, remote signals or barrier semaphores. Data moves between devices by JAX's collectives and lax.ppermute only.
A program may use at most 192 MiB of HBM per device.

```python
import jax
import jax.numpy as jnp
from jax import lax

D = 2048
HEADS = 16
FEAT = 16
HEAD_V = 128
FF = 5632
TOK_DEV = 128
SEQ_LEN = 2048
TOKENS = 16384


def draw_doc_start(key, part):
    key = jax.random.fold_in(key, 7)
    first_key, last_key, cut_key = jax.random.split(key, 3)
    row_count = TOKENS // SEQ_LEN
    first = jax.random.randint(first_key, (row_count, 1), 0, TOK_DEV)
    last = jax.random.randint(last_key, (row_count, 1), SEQ_LEN - TOK_DEV + 1, SEQ_LEN)
    positions = jnp.arange(SEQ_LEN, dtype=jnp.int32)[None, :]
    cuts = jax.random.randint(cut_key, (row_count, SEQ_LEN), 0, 16) == 0
    outside = (positions < first) | (positions > last)
    marks = (positions == 0) | (positions == first) | (positions == last) | outside & cuts
    return jnp.where(marks, 1, 0).astype(jnp.int32).reshape(row_count * SEQ_LEN)


def block_levels(own_key, extent, pieces, least, largest):
    loudness, own = 1.0, jax.random.fold_in(own_key, 6)
    for axis_at, parts in pieces:
        steps = jnp.exp(jax.random.uniform(jax.random.fold_in(own, axis_at), (parts,), jnp.float32, least / len(pieces), largest / len(pieces)))
        loudness = loudness * jnp.repeat(steps, extent[axis_at] // parts).reshape([-1 if axis == axis_at else 1 for axis in range(len(extent))])
    return loudness


def gaussian(rng, shape, spread, reach, cuts=(), held_as=jnp.bfloat16):
    values = spread * jax.random.normal(rng, shape, jnp.float32)
    if cuts:
        values = values * block_levels(rng, shape, cuts, -0.22, 0.18)
    return jnp.clip(values, -reach, reach).astype(held_as)


def setup_inputs(seed: int = 0) -> dict:
    key_list = jax.random.split(jax.random.key(seed), 13)
    return {
        "tokens": gaussian(key_list[0], (TOKENS, D), 1.0, 6.0, ((0, 128),)),
        "doc_start": draw_doc_start(jax.random.fold_in(key_list[12], 71), 0),
        "gain_first": jnp.clip(1.0 + 0.1 * jax.random.normal(key_list[2], (D,), jnp.float32), 0.5, 1.5),
        "w_query": gaussian(key_list[3], (D, HEADS * FEAT), D ** -0.5, 0.125, ((1, 16),)),
        "w_key": gaussian(key_list[4], (D, HEADS * FEAT), D ** -0.5, 0.125, ((1, 16),)),
        "w_value": gaussian(key_list[5], (D, HEADS * HEAD_V), D ** -0.5, 0.125, ((1, 16),)),
        "w_out": gaussian(key_list[6], (HEADS * HEAD_V, D), (D // 16) ** -0.5, 0.5, ((0, 16),)),
        "gain_second": jnp.clip(1.0 + 0.1 * jax.random.normal(key_list[7], (D,), jnp.float32), 0.5, 1.5),
        "w_gate": gaussian(key_list[8], (D, FF), D ** -0.5, 0.125, ((1, 16),)),
        "w_up": gaussian(key_list[9], (D, FF), D ** -0.5, 0.125, ((1, 16),)),
        "w_down": gaussian(key_list[10], (FF, D), FF ** -0.5, 0.078125, ((0, 16),)),
        "out_grad": gaussian(key_list[11], (TOKENS, D), 1.0, 6.0, ((0, 128),)),
    }


EPS = 1e-05
HIGH = lax.Precision.HIGHEST

@jax.custom_vjp
def low(v):
    return lax.optimization_barrier(v.astype(jnp.bfloat16)).astype(jnp.float32)

@jax.custom_vjp
def low_back(v):
    return v

def low_keep(v):
    return (low(v), None)

def low_pass(kept, grad):
    return (grad,)

def back_keep(v):
    return (v, None)

def back_low(kept, grad):
    return (low(grad),)
low.defvjp(low_keep, low_pass)
low_back.defvjp(back_keep, back_low)

def matmul(left, right):
    return jnp.dot(left, right, precision=HIGH, preferred_element_type=jnp.float32)

def normalize(values_in, gains):
    return values_in * lax.rsqrt(lax.optimization_barrier(jnp.mean(values_in * values_in, axis=-1, keepdims=True)) + EPS) * gains

def attend(queries, key_rows, value_rows, doc_marks):
    length = queries.shape[0]
    block_rows = min(512, length)
    doc_ids = jnp.cumsum(doc_marks, dtype=jnp.int32)
    positions = jnp.arange(length, dtype=jnp.int32)
    scaling = FEAT ** (-0.5)

    def one_block(start):
        query_block = lax.dynamic_slice_in_dim(queries, start, block_rows, 0)
        doc_block = lax.dynamic_slice_in_dim(doc_ids, start, block_rows, 0)
        row_index = start + jnp.arange(block_rows, dtype=jnp.int32)
        allowed = (positions[None, :] <= row_index[:, None]) & (doc_ids[None, :] == doc_block[:, None])
        scores = low_back(jnp.einsum('thf,shf->hts', query_block, key_rows, precision=HIGH) * scaling)
        weight = jnp.where(allowed[None], 1.0 + scores + 0.5 * scores * scores, 0.0)
        denominator = lax.optimization_barrier(jnp.sum(weight, axis=2))
        numerator = low_back(jnp.einsum('hts,shc->thc', low(weight), value_rows, precision=HIGH))
        return low(numerator / jnp.transpose(denominator)[:, :, None])
    starts = jnp.arange(length // block_rows, dtype=jnp.int32) * block_rows
    mixed_out = lax.map(jax.checkpoint(one_block), starts)
    return mixed_out.reshape(length, HEADS * HEAD_V)

def layer(x_row, doc_marks, gain_one, query_w, key_w, value_w, out_w, gain_two, gate_w, up_w, down_w):
    first_normed = low(normalize(x_row, gain_one))
    queries = low(low_back(matmul(first_normed, query_w))).reshape(SEQ_LEN, HEADS, FEAT)
    key_rows = low(low_back(matmul(first_normed, key_w))).reshape(SEQ_LEN, HEADS, FEAT)
    value_rows = low(low_back(matmul(first_normed, value_w))).reshape(SEQ_LEN, HEADS, HEAD_V)
    mixed_out = attend(queries, key_rows, value_rows, doc_marks)
    mid_rows = x_row + low_back(matmul(mixed_out, out_w))
    second_normed = low(normalize(mid_rows, gain_two))
    gate_rows = low_back(matmul(second_normed, gate_w))
    up_rows = low_back(matmul(second_normed, up_w))
    hidden = low(jax.nn.silu(gate_rows) * up_rows)
    return mid_rows + low_back(matmul(hidden, down_w))

def reference(tokens, doc_start, gain_first, w_query, w_key, w_value, w_out, gain_second, w_gate, w_up, w_down, out_grad):
    parameters = tuple((w.astype(jnp.float32) for w in (gain_first, w_query, w_key, w_value, w_out, gain_second, w_gate, w_up, w_down)))
    row_count = TOKENS // SEQ_LEN
    inputs = tokens.astype(jnp.float32).reshape(row_count, SEQ_LEN, D)
    doc_marks = doc_start.reshape(row_count, SEQ_LEN)
    cotangents = out_grad.astype(jnp.float32).reshape(row_count, SEQ_LEN, D)

    def one_row(totals, row_data):
        x_row, mark_row, cot_row = row_data

        def applied(x_in, *weights):
            return layer(x_in, mark_row, *weights)
        result, pullback = jax.vjp(applied, x_row, *parameters)
        gradients = pullback(cot_row)
        totals = tuple((a + g for a, g in zip(totals, gradients[1:])))
        return (totals, (result, gradients[0]))
    initial = tuple((jnp.zeros_like(w) for w in parameters))
    totals, (outputs, input_grads) = lax.scan(one_row, initial, (inputs, doc_marks, cotangents))
    return (outputs.reshape(TOKENS, D), input_grads.reshape(TOKENS, D), totals[0], totals[1], totals[2], totals[3], totals[4], totals[5], totals[6], totals[7], totals[8])
```

```python
import jax
import jax.numpy as jnp
from jax import lax
from jax.experimental import pallas as pl
from jax.experimental.pallas import tpu as pltpu
from jax.sharding import Mesh, PartitionSpec as P

FEAT = 16
HEAD_V = 128
EPS = 1e-05
F32 = jnp.float32
BF16 = jnp.bfloat16
TOK = 128
GROUP = 512
SEQ = 2048
HEAD_ROWS = 2 * FEAT + HEAD_V
AXES = ("x", "core", "z", "y")
D = 2048
HID = 352
PIECE = 256


def shifted(array, axis, by):
    return lax.ppermute(array, axis, [(i, (i + by) % 4) for i in range(4)])


def swapped(array):
    return lax.ppermute(array, "core", [(0, 1), (1, 0)])


def gathered(array, axis):
    return [
        array,
        shifted(array, axis, 3),
        shifted(array, axis, 2),
        shifted(array, axis, 1),
    ]


def ring_gathered(array, axis):
    half = array.shape[0] // 2
    ahead, back = shifted(array, axis, 3), shifted(array, axis, 1)
    return [array, ahead, shifted(back[:half], axis, 1), shifted(ahead[half:], axis, 3), back]


def ring_start(opposite, axis):
    return shifted(opposite[0], axis, 1), shifted(opposite[1], axis, 3)


def ring_end(arrived, ahead, back, axis):
    half = ahead.shape[0] // 2
    first, second = arrived
    ahead = jnp.concatenate([ahead[:half] + first, ahead[half:]], axis=0)
    back = jnp.concatenate([back[:half], back[half:] + second], axis=0)
    return shifted(ahead, axis, 1), shifted(back, axis, 3)


def exchanged(blocks, axis):
    return [
        blocks[0],
        shifted(blocks[1], axis, 1),
        shifted(blocks[2], axis, 2),
        shifted(blocks[3], axis, 3),
    ]


def in_order(blocks, at):
    stacked = jnp.stack(blocks)
    return jnp.concatenate(
        [lax.dynamic_index_in_dim(stacked, (j - at) % 4, 0, keepdims=False) for j in range(4)], axis=0
    )


def nn(left, right):
    return jnp.dot(left, right, preferred_element_type=F32)


def nt(left, right):
    return lax.dot_general(left, right, (((1,), (1,)), ((), ())), preferred_element_type=F32)


def tn(left, right):
    return lax.dot_general(left, right, (((0,), (0,)), ((), ())), preferred_element_type=F32)


def pair_mask(start_row, si, ti, first, rows):
    row = lax.broadcasted_iota(jnp.int32, (rows, GROUP), 0) + (si * GROUP + first)
    mask = row >= start_row
    if si == ti:
        column = lax.broadcasted_iota(jnp.int32, (rows, GROUP), 1) + ti * GROUP
        mask = mask & (row <= column)
    return mask


def forward_kernel(
    at_ref, q0, q1, q2, q3, start_ref, mixed_ref, numer_ref, denom_ref, qkv_ref, keys
):
    for d, ref in enumerate((q0, q1, q2, q3)):
        qkv_ref[(at_ref[2] + 4 - d) % 4] = ref[...]
    for si in range(4):
        keys[si] = jnp.transpose(qkv_ref[si, FEAT : 2 * FEAT, :].astype(F32)).astype(BF16)
    for ti in range(4):
        query = (qkv_ref[ti, 0:FEAT, :].astype(F32) * (FEAT**-0.5)).astype(BF16)
        start_row = start_ref[:, ti * GROUP : (ti + 1) * GROUP]
        numer = jnp.zeros((HEAD_V, GROUP), F32)
        denom = jnp.zeros((1, GROUP), F32)
        for si in range(ti + 1):
            one = nn(keys[si], query) + 1.0
            weight = jnp.where(
                pair_mask(start_row, si, ti, 0, GROUP), 0.5 * (one * one) + 0.5, 0.0
            )
            denom = denom + jnp.sum(weight, axis=0, keepdims=True)
            numer = numer + nn(qkv_ref[si, 2 * FEAT :, :], weight.astype(BF16))
        numer_ref[ti] = numer
        denom_ref[ti] = denom
        mixed = (numer / denom).astype(BF16)
        for j in range(4):
            mixed_ref[ti * 4 + j] = mixed[:, j * TOK : (j + 1) * TOK]


def attention_forward(order, at, qkv, start_row, wait):
    return order.call(
        forward_kernel,
        "attention_forward",
        (
            jax.ShapeDtypeStruct((16, HEAD_V, TOK), BF16),
            jax.ShapeDtypeStruct((4, HEAD_V, GROUP), F32),
            jax.ShapeDtypeStruct((4, 1, GROUP), F32),
            like(4, HEAD_ROWS, GROUP),
        ),
        (at, *qkv, start_row),
        [pltpu.VMEM((4, GROUP, FEAT), BF16)],
        wait,
        in_specs=[SMEM] + [WHOLE] * 5,
        out_specs=(WHOLE,) * 4,
    )


def backward_kernel(
    at_ref,
    qkv_ref,
    cot_ref,
    numer_ref,
    denom_ref,
    start_ref,
    g0,
    g1,
    g2,
    g3,
    out_ref,
    keys,
    values,
    key_sum,
    value_sum,
):
    for si in range(4):
        keys[si] = jnp.transpose(qkv_ref[si, FEAT : 2 * FEAT, :].astype(F32)).astype(BF16)
        values[si] = jnp.transpose(qkv_ref[si, 2 * FEAT :, :].astype(F32)).astype(BF16)
    key_sum[...] = jnp.zeros_like(key_sum)
    value_sum[...] = jnp.zeros_like(value_sum)
    for ti in range(4):
        query_f32 = qkv_ref[ti, 0:FEAT, :].astype(F32) * (FEAT**-0.5)
        query = query_f32.astype(BF16)
        query_rows = jnp.transpose(query_f32).astype(BF16)
        start_row = start_ref[:, ti * GROUP : (ti + 1) * GROUP]
        inverse = 1.0 / denom_ref[ti]
        cot = jnp.concatenate([cot_ref[ti * 4 + j] for j in range(4)], axis=1).astype(F32)
        cot_denom = -jnp.sum(cot * numer_ref[ti], axis=0, keepdims=True) * (inverse * inverse)
        cot_f32 = cot * inverse
        cot_numer = cot_f32.astype(BF16)
        cot_rows = jnp.transpose(cot_f32).astype(BF16)
        query_sum = jnp.zeros((FEAT, GROUP), F32)
        for si in range(ti + 1):
            one = nn(keys[si], query) + 1.0
            mask = pair_mask(start_row, si, ti, 0, GROUP)
            weight = jnp.where(mask, 0.5 * (one * one) + 0.5, 0.0).astype(BF16)
            value_sum[si] += nn(weight, cot_rows)
            cot_weight = nn(values[si], cot_numer) + cot_denom
            cot_score = jnp.where(mask, cot_weight * one, 0.0).astype(BF16)
            key_sum[si] += nn(cot_score, query_rows)
            query_sum = query_sum + nn(qkv_ref[si, FEAT : 2 * FEAT, :], cot_score)
        out_ref[ti, 0:FEAT, :] = (query_sum * (FEAT**-0.5)).astype(BF16)
    for si in range(4):
        out_ref[si, FEAT : 2 * FEAT, :] = jnp.transpose(key_sum[si]).astype(BF16)
        out_ref[si, 2 * FEAT :, :] = jnp.transpose(value_sum[si]).astype(BF16)
    for d, ref in enumerate((g0, g1, g2, g3)):
        ref[...] = out_ref[(at_ref[2] + d) % 4]


def attention_backward(order, at, qkv, cot, numer, denom, start_row):
    return order.call(
        backward_kernel,
        "attention_backward",
        (like(HEAD_ROWS, GROUP),) * 4,
        (at, qkv, cot, numer, denom, start_row),
        [
            pltpu.VMEM((4, HEAD_ROWS, GROUP), BF16),
            pltpu.VMEM((4, GROUP, FEAT), BF16),
            pltpu.VMEM((4, GROUP, HEAD_V), BF16),
            pltpu.VMEM((4, GROUP, FEAT), F32),
            pltpu.VMEM((4, GROUP, HEAD_V), F32),
        ],
        in_specs=[SMEM] + [WHOLE] * 5,
        out_specs=(WHOLE,) * 4,
    )


VMEM_LIMIT = 52 * 2**20


class Order:
    def __init__(self):
        self.last = ()

    def call(self, kernel, name, out_shape, args, scratch=(), wait=(), **specs):
        at, first, *rest = args
        first = lax.optimization_barrier((first, *self.last, *wait))[0]
        out = pl.pallas_call(
            kernel,
            out_shape=out_shape,
            scratch_shapes=list(scratch),
            compiler_params=pltpu.CompilerParams(vmem_limit_bytes=VMEM_LIMIT),
            cost_estimate=pl.CostEstimate(flops=1, bytes_accessed=1, transcendentals=0),
            name=name,
            **specs,
        )(at, first, *rest)
        self.last = (out[0] if isinstance(out, (tuple, list)) else out,)
        return out


SMEM = pl.BlockSpec(memory_space=pltpu.SMEM)
WHOLE = pl.BlockSpec(memory_space=pltpu.VMEM)


def spec(*shape, at=None):
    def index(i):
        return tuple(i if k == at else 0 for k in range(len(shape)))

    return pl.BlockSpec(shape, index)


def like(*shape, dtype=BF16):
    return jax.ShapeDtypeStruct(shape, dtype)


def piece_at(at_ref, place, own_core):
    core = at_ref[1] if own_core else 1 - at_ref[1]
    return pl.multiple_of(((at_ref[0] + place) % 4 * 2 + core) * PIECE, PIECE)


def inverse_rms(rows):
    return lax.rsqrt(jnp.mean(rows * rows, axis=1, keepdims=True) + EPS)


def norm_back(grad_normed, unit, inverse, gains):
    scaled = grad_normed * gains
    return inverse * (scaled - unit * jnp.mean(scaled * unit, axis=1, keepdims=True))


RING_ROWS = ((0, 0, TOK), (1, 0, TOK), (2, 0, TOK // 2), (2, TOK // 2, TOK // 2), (3, 0, TOK))


def project_kernel(at_ref, *refs):
    tokens, weights, gain_ref = refs[:5], refs[5:10], refs[10]
    outs, normed_ref = refs[11:15], refs[15]
    for token_ref, (d, first, count) in zip(tokens, RING_ROWS):
        rows = token_ref[...].astype(F32)
        normed = (rows * inverse_rms(rows) * gain_ref[...]).astype(BF16)
        at = pl.multiple_of((at_ref[3] + d) % 4 * TOK, TOK) + first
        normed_ref[pl.ds(pl.multiple_of(at, count), count), :] = normed
    normed = normed_ref[...]
    half = HEAD_ROWS // 2
    for d, w_ref in ((0, weights[0]), (1, weights[1]), (3, weights[4])):
        outs[d][...] = nt(w_ref[...], normed).astype(BF16)
    outs[2][:half, :] = nt(weights[2][...], normed).astype(BF16)
    outs[2][half:, :] = nt(weights[3][...], normed).astype(BF16)


def project(order, at, token_blocks, head_blocks, gain, wait):
    return order.call(
        project_kernel,
        "project",
        (like(HEAD_ROWS, GROUP),) * 4 + (like(GROUP, D),),
        (at, *token_blocks, *head_blocks, gain[None, :]),
        wait=wait,
        in_specs=[SMEM] + [WHOLE] * 11,
        out_specs=(WHOLE,) * 5,
    )


def half_at(at_ref, own):
    core = at_ref[1] if own else 1 - at_ref[1]
    return pl.ds(pl.multiple_of(core * 1024, 1024), 1024)


def middle_kernel(at_ref, mixed_ref, token_ref, gain_ref, own_ref, other_ref, mid_ref, normed_ref):
    mixed = jnp.transpose(mixed_ref[...].astype(F32)).astype(BF16)
    for own, w_ref in ((True, own_ref), (False, other_ref)):
        columns = half_at(at_ref, own)
        mid_ref[:, columns] = token_ref[:, columns].astype(F32) + nn(mixed, w_ref[...])
    mid = mid_ref[...]
    normed_ref[...] = (mid * inverse_rms(mid) * gain_ref[...]).astype(BF16)


def middle(order, at, mixed, tokens, gain, weights):
    return order.call(
        middle_kernel,
        "middle",
        (like(TOK, D, dtype=F32), like(TOK, D)),
        (at, mixed, tokens, gain[None, :], *weights),
        in_specs=[SMEM] + [WHOLE] * 5,
        out_specs=(WHOLE, WHOLE),
    )


RING = ((0, TOK), (TOK, TOK), (2 * TOK, TOK // 2), (2 * TOK + TOK // 2, TOK // 2), (3 * TOK, TOK))
RING_SPECS = [spec(count, D) for _, count in RING]
RING_LIKE = tuple(like(count, D) for _, count in RING)


def feed_kernel(at_ref, *refs):
    blocks, cot_refs, gu_mine, gu_other = refs[:5], refs[5:10], refs[10], refs[11]
    down_refs, (hidden_ref, gate_ref, up_ref) = refs[12:20], refs[20:23]
    outs, (rows, cots, downs, total) = refs[23:28], refs[28:]
    step = pl.program_id(0)

    @pl.when(step == 0)
    def _():
        for (first, count), block, cot_ref in zip(RING, blocks, cot_refs):
            at = slice(first, first + count)
            for own in (0, 1):
                rows[own, at, :] = block[:, half_at(at_ref, own == 0)]
                for d in range(4):
                    columns = pl.ds(piece_at(at_ref, d, own == 0), PIECE)
                    piece = own * 4 + d
                    cots[at, piece * PIECE : (piece + 1) * PIECE] = cot_ref[:, columns]

    weights = (gu_mine, gu_other)
    for d, w_ref in enumerate(down_refs):
        downs[:, d * PIECE : (d + 1) * PIECE] = w_ref[0]
    both_rows = nt(gu_mine[0], rows[0]) + nt(gu_other[0], rows[1])
    gate_rows, up_rows = both_rows[:HID], both_rows[HID:]
    grad_hidden = nt(downs[...], cots[...])
    sigmoid_gate = 1.0 / (1.0 + jnp.exp(-gate_rows))
    silu_gate = gate_rows * sigmoid_gate
    hidden_ref[0] = (silu_gate * up_rows).astype(BF16)
    up_delta = (grad_hidden * silu_gate).astype(BF16)
    gate_delta = (
        grad_hidden * up_rows * (sigmoid_gate + silu_gate * (1.0 - sigmoid_gate))
    ).astype(BF16)
    gate_ref[0] = gate_delta
    up_ref[0] = up_delta
    both_delta = jnp.concatenate([gate_delta, up_delta], axis=0)
    for own in (0, 1):
        part = tn(both_delta, weights[own][0])

        @pl.when(step == 0)
        def _():
            total[own] = part

        @pl.when(step > 0)
        def _():
            total[own] += part

    @pl.when(step == 3)
    def _():
        for (first, count), out_ref in zip(RING, outs):
            for own in (0, 1):
                out_ref[:, half_at(at_ref, own == 0)] = total[
                    own, first : first + count, :
                ].astype(BF16)


def feed(order, at, second_blocks, cot_blocks, gu_mine, gu_other, down_pieces, wait):
    deltas = like(4, HID, GROUP)
    return order.call(
        feed_kernel,
        "feed",
        (deltas, deltas, deltas) + RING_LIKE,
        (at, *second_blocks, *cot_blocks, gu_mine, gu_other, *down_pieces),
        [
            pltpu.VMEM((2, GROUP, 1024), BF16),
            pltpu.VMEM((GROUP, D), BF16),
            pltpu.VMEM((HID, D), BF16),
            pltpu.VMEM((2, GROUP, 1024), F32),
        ],
        wait,
        grid=(4,),
        in_specs=[SMEM]
        + RING_SPECS * 2
        + [spec(1, 2 * HID, 1024, at=0)] * 2
        + [spec(1, HID, PIECE, at=0)] * 8,
        out_specs=(spec(1, HID, GROUP, at=0),) * 3 + tuple(RING_SPECS),
    )


def down_kernel(at_ref, hidden_ref, *refs):
    weights, outs, rows = refs[:8], refs[8:13], refs[13]
    for z in range(4):
        rows[z] = jnp.transpose(hidden_ref[z].astype(F32)).astype(BF16)
    for d in range(8):
        part = nn(rows[0], weights[d][0])
        for z in range(1, 4):
            part = part + nn(rows[z], weights[d][z])
        columns = pl.ds(piece_at(at_ref, d % 4, d < 4), PIECE)
        for (first, count), out_ref in zip(RING, outs):
            out_ref[:, columns] = part[first : first + count].astype(BF16)


def down(order, at, hidden, down_pieces):
    return order.call(
        down_kernel,
        "down",
        RING_LIKE,
        (at, hidden, *down_pieces),
        [pltpu.VMEM((4, GROUP, HID), BF16)],
        in_specs=[SMEM] + [WHOLE] * 9,
        out_specs=(WHOLE,) * 5,
    )


def feed_grads_kernel(own, count, at_ref, *refs):
    lefts, blocks, others = refs[:count], refs[count : count + 5], refs[count + 5 : -2]
    out_ref, rows = refs[-2:]
    step = pl.program_id(0)

    @pl.when(step == 0)
    def _():
        core = at_ref[1] if own else 1 - at_ref[1]
        for (first, size), block in zip(RING, blocks):
            for k in range(4):
                columns = pl.ds(pl.multiple_of((k * 2 + core) * PIECE, PIECE), PIECE)
                rows[first : first + size, k * PIECE : (k + 1) * PIECE] = block[:, columns]

    for i, left_ref in enumerate(lefts):
        part = nn(left_ref[0], rows[...])
        for k in range(4):
            block = part[:, k * PIECE : (k + 1) * PIECE]
            if own:
                block = block + others[0][k, 0, i * HID : (i + 1) * HID, :].astype(F32)
            out_ref[k, 0, i * HID : (i + 1) * HID, :] = block.astype(BF16)


def feed_grads(order, at, lefts, blocks, other=None, wait=()):
    own, count = other is not None, len(lefts)
    grads = spec(4, 1, count * HID, PIECE, at=1)
    return order.call(
        lambda *refs: feed_grads_kernel(own, count, *refs),
        "feed_grads_own" if own else "feed_grads",
        like(4, 4, count * HID, PIECE),
        (at, *lefts, *blocks) + ((other,) if own else ()),
        [pltpu.VMEM((GROUP, 1024), BF16)],
        wait,
        grid=(4,),
        in_specs=[SMEM]
        + [spec(1, HID, GROUP, at=0)] * count
        + RING_SPECS
        + ([grads] if own else []),
        out_specs=grads,
    )


def turn_kernel(
    at_ref,
    s0,
    s1,
    s3,
    mid_ref,
    cot_ref,
    gain_ref,
    own_ref,
    other_ref,
    grad_mid_ref,
    branch_ref,
    mixed_ref,
    gain_part_ref,
):
    grad_second = s0[...].astype(F32) + s1[...].astype(F32) + s3[...].astype(F32)
    mid = mid_ref[...]
    inverse = inverse_rms(mid)
    unit = mid * inverse
    gain_part_ref[...] = jnp.sum(grad_second * unit, axis=0, keepdims=True)
    grad_mid = cot_ref[...].astype(F32) + norm_back(grad_second, unit, inverse, gain_ref[...])
    grad_mid_ref[...] = grad_mid
    branch_ref[...] = grad_mid.astype(BF16)
    total = nt(own_ref[...], branch_ref[:, half_at(at_ref, True)])
    total = total + nt(other_ref[...], branch_ref[:, half_at(at_ref, False)])
    mixed_ref[...] = total.astype(BF16)


def turn(order, at, second_sums, mid_rows, out_grad, gain, weights):
    return order.call(
        turn_kernel,
        "turn",
        (
            like(TOK, D, dtype=F32),
            like(TOK, D),
            like(D, TOK),
            like(1, D, dtype=F32),
        ),
        (at, *second_sums, mid_rows, out_grad, gain[None, :], *weights),
        in_specs=[SMEM] + [WHOLE] * 8,
        out_specs=(WHOLE,) * 4,
    )


def split_pieces(at_ref, rows, d, mine_ref, other_ref):
    for k in range(4):
        low = rows[:, 2 * k * PIECE : (2 * k + 1) * PIECE]
        high = rows[:, (2 * k + 1) * PIECE : (2 * k + 2) * PIECE]
        first = at_ref[1] == 0
        count = rows.shape[0]
        mine_ref[d, k, :count] = jnp.where(first, low, high).astype(BF16)
        other_ref[d, k, :count] = jnp.where(first, high, low).astype(BF16)


def out_grads_kernel(at_ref, m0, m1, m2, m3, b0, b1, b2a, b2b, b3, mine_ref, other_ref, rows):
    for (first, count), block_ref in zip(RING, (b0, b1, b2a, b2b, b3)):
        rows[first : first + count, :] = block_ref[...]
    for back, mixed_ref in enumerate((m0, m1, m2, m3)):
        mixed = jnp.concatenate([mixed_ref[(at_ref[3] + d) % 4] for d in range(4)], axis=1)
        split_pieces(at_ref, nn(mixed, rows[...]), (4 - back) % 4, mine_ref, other_ref)


def out_grads(order, at, mixed_heads, branch_blocks):
    return order.call(
        out_grads_kernel,
        "out_grads",
        (like(4, 4, HEAD_V, PIECE), like(4, 4, HEAD_V, PIECE)),
        (at, *mixed_heads, *branch_blocks),
        [pltpu.VMEM((GROUP, D), BF16)],
        in_specs=[SMEM] + [WHOLE] * 9,
        out_specs=(WHOLE, WHOLE),
    )


BOTH_ROWS = HEAD_ROWS + HEAD_V


def head_grads_kernel(
    at_ref, g0, g1, g2, g3, normed_ref, out_mine, out_other, mine_ref, other_ref
):
    for back, grads_ref in enumerate((g0, g1, g2, g3)):
        part = nn(grads_ref[...], normed_ref[...])
        split_pieces(at_ref, part, (4 - back) % 4, mine_ref, other_ref)
    mine_ref[:, :, HEAD_ROWS:, :] = out_mine[...]
    other_ref[:, :, HEAD_ROWS:, :] = out_other[...]


def head_grads(order, at, grads, normed, outs):
    both = like(4, 4, BOTH_ROWS, PIECE)
    return order.call(
        head_grads_kernel,
        "head_grads",
        (both, both),
        (at, *grads, normed, *outs),
        in_specs=[SMEM] + [WHOLE] * 7,
        out_specs=(WHOLE, WHOLE),
    )


def first_kernel(at_ref, *refs):
    grads, (w0, w1, w2a, w2b, w3), tokens = refs[:4], refs[4:9], refs[9:14]
    outs, gain_ref = refs[14:19], refs[19]
    half = HEAD_ROWS // 2
    gain_part = jnp.zeros((1, D), F32)
    for token_ref, out_ref, (d, first, count) in zip(tokens, outs, RING_ROWS):
        columns = pl.ds(pl.multiple_of((at_ref[3] + d) % 4 * TOK, TOK), TOK)
        part = tn(grads[0][:, columns], w0[...]) + tn(grads[3][:, columns], w1[...])
        part = part + tn(grads[1][:, columns], w3[...])
        part = part + tn(grads[2][:half, columns], w2a[...])
        part = part + tn(grads[2][half:, columns], w2b[...])
        part = part[first : first + count]
        rows = token_ref[...].astype(F32)
        gain_part = gain_part + jnp.sum(part * (rows * inverse_rms(rows)), axis=0, keepdims=True)
        out_ref[...] = part.astype(BF16)
    gain_ref[...] = gain_part


def first_part(order, at, grads, head_blocks, token_blocks):
    return order.call(
        first_kernel,
        "first_part",
        RING_LIKE + (like(1, D, dtype=F32),),
        (at, *grads, *head_blocks, *token_blocks),
        in_specs=[SMEM] + [WHOLE] * 14,
        out_specs=(WHOLE,) * 6,
    )


def collect_kernel(at_ref, *refs):
    outs = refs[8:]
    for own in (True, False):
        for d in range(4):
            columns = pl.ds(piece_at(at_ref, d, own), PIECE)
            first = 0
            for out_ref in outs:
                rows = out_ref.shape[0]
                block = refs[d if own else 4 + d][first : first + rows, :]
                out_ref[:, columns] = block.astype(F32)
                first += -rows // 16 * -16


def collect(order, at, mine, name, *rows):
    other = [swapped(block) for block in mine]
    return order.call(
        collect_kernel,
        name,
        tuple(like(r, D, dtype=F32) for r in rows),
        (at, *mine, *other),
        in_specs=[SMEM] + [WHOLE] * 8,
        out_specs=(WHOLE,) * len(rows),
    )


def after(array, *needed):
    return lax.optimization_barrier((array, *needed))[0]


def body(
    tokens,
    doc_start,
    gain_first,
    w_query,
    w_key,
    w_value,
    w_out,
    gain_second,
    w_gate,
    w_up,
    w_down,
    out_grad,
):
    order = Order()
    at = jnp.stack([lax.axis_index(a) for a in AXES]).astype(jnp.int32)
    x_at, core, z_at, y_at = (at[i] for i in range(4))

    token_blocks = ring_gathered(tokens, "y")
    w_head = jnp.concatenate([w_query.T, w_key.T, w_value.T], axis=0)
    head_blocks = ring_gathered(w_head, "z")
    out_half = lax.dynamic_slice_in_dim(w_out, core * 1024, 1024, 1)
    out_mine = lax.all_gather(out_half, ("z", "y"), axis=0, tiled=True)
    piece = lax.dynamic_slice_in_dim(w_down, (x_at * 2 + core) * PIECE, PIECE, 1)
    gate_up = jnp.concatenate([w_gate.T, w_up.T], axis=0)
    gate_up = lax.dynamic_slice_in_dim(gate_up, core * 1024, 1024, 1)
    *qkv, group_normed = project(order, at, token_blocks, head_blocks, gain_first, ())
    qkv = exchanged(qkv, "z")
    gu_mine = lax.all_gather(after(gate_up, *qkv), "z", axis=0)
    down_piece = in_order([b[None] for b in gathered(piece, "z")], z_at)
    down_mine = gathered(down_piece, "x")
    cot_blocks = ring_gathered(out_grad, "y")

    positions = jnp.arange(SEQ, dtype=jnp.int32)
    start_row = lax.cummax(jnp.where(doc_start != 0, positions, 0))[None, :]
    mixed, numer, denom, qkv = attention_forward(order, at, qkv, start_row, ())
    mixed_tokens = lax.all_to_all(mixed, ("z", "y"), 0, 0).reshape(SEQ, TOK)
    out_mine = after(out_mine, mixed)
    out_weights = (out_mine, swapped(out_mine))
    mid_rows, second_normed = middle(order, at, mixed_tokens, tokens, gain_second, out_weights)

    second_blocks = ring_gathered(second_normed, "y")
    mixed_groups = mixed.reshape(4, 4, HEAD_V, TOK)
    mixed_heads = exchanged(
        [lax.dynamic_index_in_dim(mixed_groups, (z_at + d) % 4, 0, False) for d in range(4)], "z"
    )
    gu_mine, *down_mine, _ = lax.optimization_barrier((gu_mine, *down_mine, second_normed))
    gu_other = swapped(gu_mine)
    down_pieces = [*down_mine, *(swapped(b) for b in down_mine)]
    hidden, gate_delta, up_delta, s0, s1, *s2, s3 = feed(
        order, at, second_blocks, cot_blocks, gu_mine, gu_other, down_pieces, mixed_heads
    )
    arrived = ring_start(s2, "y")
    second_sums = (s0, *ring_end(arrived, s1, s3, "y"))
    gu_grads = swapped(
        feed_grads(order, at, (gate_delta, up_delta), second_blocks, wait=arrived)
    )
    b0, b1, *b2, b3 = down(order, at, hidden, down_pieces)
    gu_grads = feed_grads(order, at, (gate_delta, up_delta), second_blocks, gu_grads)
    gu_sum = lax.psum_scatter(
        gu_grads.reshape(16, 2 * HID, PIECE), ("x", "z"), scatter_dimension=0
    )

    grad_mid, grad_branch, grad_mixed, gain_second_part = turn(
        order, at, second_sums, mid_rows, out_grad, gain_second, out_weights
    )
    grad_mixed = lax.all_to_all(grad_mixed.reshape(16, HEAD_V, TOK), ("z", "y"), 0, 0)
    branch_blocks = ring_gathered(grad_branch, "y")
    down_grads = swapped(feed_grads(order, at, (hidden,), cot_blocks))
    down_grads = feed_grads(order, at, (hidden,), cot_blocks, down_grads)
    down_grads = [
        lax.dynamic_index_in_dim(down_grads, (z_at + d) % 4, 1, False) for d in range(4)
    ]
    grads = attention_backward(order, at, qkv, grad_mixed, numer, denom, start_row)
    grads = exchanged(grads, "z")

    def added(blocks):
        total = (blocks[0].astype(F32) + blocks[1].astype(F32)) + (
            blocks[2].astype(F32) + blocks[3].astype(F32)
        )
        return total.astype(BF16)

    def summed(blocks):
        part = added(exchanged(blocks, "z"))
        return added(
            exchanged(
                [lax.dynamic_index_in_dim(part, (x_at + d) % 4, 0, False) for d in range(4)], "x"
            )
        )

    down_sum = summed(down_grads)
    outs = out_grads(order, at, mixed_heads, branch_blocks)
    f0, f1, *f2, f3, gain_first_part = first_part(order, at, grads, head_blocks, token_blocks)
    from_back, from_ahead = ring_end(ring_start(f2, "y"), f1, f3, "y")
    mine, other = head_grads(order, at, grads, group_normed, outs)
    gains = jnp.concatenate([gain_first_part, gain_second_part], axis=0)
    blocks = gathered(gains, "y")
    gains = (blocks[0] + blocks[1]) + (blocks[2] + blocks[3])
    gains = (gains + swapped(gains)).astype(BF16).reshape(2, 4, 2, PIECE)
    gains = lax.dynamic_index_in_dim(gains, core, 2, False)
    gains = jnp.pad(jnp.transpose(gains, (1, 0, 2)), ((0, 0), (0, 14), (0, 0)))
    both = (mine.astype(F32) + swapped(other).astype(F32)).astype(BF16)
    head_sum = summed([jnp.concatenate([both[d], gains], axis=1) for d in range(4)])

    grad_first = f0.astype(F32) + from_back.astype(F32) + from_ahead.astype(F32)
    b_back, b_ahead = ring_end(ring_start(b2, "y"), b1, b3, "y")
    block_out = mid_rows + (b0.astype(F32) + b_back.astype(F32) + b_ahead.astype(F32))
    x_rows = tokens.astype(F32)
    first_inv = inverse_rms(x_rows)
    input_grad = grad_mid + norm_back(grad_first, x_rows * first_inv, first_inv, gain_first)

    ffn_sum = jnp.concatenate([gu_sum, down_sum], axis=0)
    grad_gate, grad_up, grad_down = collect(
        order, at, gathered(ffn_sum, "x"), "collect_feed", HID, HID, HID
    )
    grad_query, grad_key, grad_value, grad_out, gains = collect(
        order, at, gathered(head_sum, "x"), "collect_heads", FEAT, FEAT, HEAD_V, HEAD_V, 2
    )
    return (
        block_out,
        input_grad,
        gains[0],
        grad_query.T,
        grad_key.T,
        grad_value.T,
        grad_out,
        gains[1],
        grad_gate.T,
        grad_up.T,
        grad_down,
    )


def solution(mesh):
    fine = Mesh(mesh.devices.reshape(4, 2, 4, 4), AXES)
    rows, dp, mp = P(AXES, None), P(("x", "core")), ("z", "y")
    return jax.shard_map(
        body,
        mesh=fine,
        in_specs=(
            rows,
            dp,
            P(),
            P(None, mp),
            P(None, mp),
            P(None, mp),
            P(mp, None),
            P(),
            P(None, mp),
            P(None, mp),
            P(mp, None),
            rows,
        ),
        out_specs=(
            rows,
            rows,
            P(),
            P(None, mp),
            P(None, mp),
            P(None, mp),
            P(mp, None),
            P(),
            P(None, mp),
            P(None, mp),
            P(mp, None),
        ),
        check_vma=False,
    )
```

```python
import jax
import jax.numpy as jnp
from jax import lax
from jax.experimental import pallas as pl
from jax.experimental.pallas import tpu as pltpu
from jax.sharding import Mesh, PartitionSpec as P

FEAT = 16
HEAD_V = 128
EPS = 1e-05
F32 = jnp.float32
BF16 = jnp.bfloat16
TOK = 128
GROUP = 512
SEQ = 2048
HEAD_ROWS = 2 * FEAT + HEAD_V
AXES = ("x", "core", "z", "y")
D = 2048
HID = 352
PIECE = 256


def shifted(array, axis, by):
    return lax.ppermute(array, axis, [(i, (i + by) % 4) for i in range(4)])


def swapped(array):
    return lax.ppermute(array, "core", [(0, 1), (1, 0)])


def swapped_each(arrays):
    return [swapped(array) for array in arrays]


def gathered(array, axis):
    return [
        array,
        shifted(array, axis, 3),
        shifted(array, axis, 2),
        shifted(array, axis, 1),
    ]


def ring_gathered(array, axis):
    half = array.shape[0] // 2
    ahead, back = shifted(array, axis, 3), shifted(array, axis, 1)
    return [array, ahead, shifted(back[:half], axis, 1), shifted(ahead[half:], axis, 3), back]


def ring_start(opposite, axis):
    return shifted(opposite[0], axis, 1), shifted(opposite[1], axis, 3)


def ring_end(arrived, ahead, back, axis):
    half = ahead.shape[0] // 2
    first, second = arrived
    ahead = jnp.concatenate([ahead[:half] + first, ahead[half:]], axis=0)
    back = jnp.concatenate([back[:half], back[half:] + second], axis=0)
    return shifted(ahead, axis, 1), shifted(back, axis, 3)


def exchanged(blocks, axis):
    return [
        blocks[0],
        shifted(blocks[1], axis, 1),
        shifted(blocks[2], axis, 2),
        shifted(blocks[3], axis, 3),
    ]


def in_order(blocks, at):
    stacked = jnp.stack(blocks)
    return jnp.concatenate(
        [lax.dynamic_index_in_dim(stacked, (j - at) % 4, 0, keepdims=False) for j in range(4)], axis=0
    )


def nn(left, right):
    return jnp.dot(left, right, preferred_element_type=F32)


def nt(left, right):
    return lax.dot_general(left, right, (((1,), (1,)), ((), ())), preferred_element_type=F32)


def tn(left, right):
    return lax.dot_general(left, right, (((0,), (0,)), ((), ())), preferred_element_type=F32)


def pair_mask(start_row, si, ti, first, rows):
    row = lax.broadcasted_iota(jnp.int32, (rows, GROUP), 0) + (si * GROUP + first)
    mask = row >= start_row
    if si == ti:
        column = lax.broadcasted_iota(jnp.int32, (rows, GROUP), 1) + ti * GROUP
        mask = mask & (row <= column)
    return mask


def forward_kernel(
    at_ref,
    q0,
    q1,
    q2,
    q3,
    start_ref,
    m0,
    m1,
    m2,
    m3,
    numer_ref,
    denom_ref,
    qkv_ref,
    mixed_ref,
    keys,
):
    for d, ref in enumerate((q0, q1, q2, q3)):
        qkv_ref[(at_ref[2] + 4 - d) % 4] = ref[...]
    for si in range(4):
        keys[si] = jnp.transpose(qkv_ref[si, FEAT : 2 * FEAT, :].astype(F32)).astype(BF16)
    for ti in range(4):
        query = (qkv_ref[ti, 0:FEAT, :].astype(F32) * (FEAT**-0.5)).astype(BF16)
        start_row = start_ref[:, ti * GROUP : (ti + 1) * GROUP]
        numer = jnp.zeros((HEAD_V, GROUP), F32)
        denom = jnp.zeros((1, GROUP), F32)
        for si in range(ti + 1):
            one = nn(keys[si], query) + 1.0
            weight = jnp.where(
                pair_mask(start_row, si, ti, 0, GROUP), 0.5 * (one * one) + 0.5, 0.0
            )
            denom = denom + jnp.sum(weight, axis=0, keepdims=True)
            numer = numer + nn(qkv_ref[si, 2 * FEAT :, :], weight.astype(BF16))
        numer_ref[ti] = numer
        denom_ref[ti] = denom
        mixed_ref[ti] = (numer / denom).astype(BF16)
    for d, ref in enumerate((m0, m1, m2, m3)):
        ref[...] = mixed_ref[(at_ref[2] + d) % 4]


def attention_forward(order, at, qkv, start_row, wait):
    return order.call(
        forward_kernel,
        "attention_forward",
        (like(HEAD_V, GROUP),) * 4
        + (
            like(4, HEAD_V, GROUP, dtype=F32),
            like(4, 1, GROUP, dtype=F32),
            like(4, HEAD_ROWS, GROUP),
        ),
        (at, *qkv, start_row),
        [pltpu.VMEM((4, HEAD_V, GROUP), BF16), pltpu.VMEM((4, GROUP, FEAT), BF16)],
        wait,
        in_specs=[SMEM] + [WHOLE] * 5,
        out_specs=(WHOLE,) * 7,
    )


def backward_kernel(
    at_ref,
    c0,
    c1,
    c2,
    c3,
    qkv_ref,
    numer_ref,
    denom_ref,
    start_ref,
    g0,
    g1,
    g2,
    g3,
    out_ref,
    cot_ref,
    keys,
    values,
    key_sum,
    value_sum,
):
    for d, ref in enumerate((c0, c1, c2, c3)):
        cot_ref[(at_ref[2] + 4 - d) % 4] = ref[...]
    for si in range(4):
        keys[si] = jnp.transpose(qkv_ref[si, FEAT : 2 * FEAT, :].astype(F32)).astype(BF16)
        values[si] = jnp.transpose(qkv_ref[si, 2 * FEAT :, :].astype(F32)).astype(BF16)
    key_sum[...] = jnp.zeros_like(key_sum)
    value_sum[...] = jnp.zeros_like(value_sum)
    for ti in range(4):
        query_f32 = qkv_ref[ti, 0:FEAT, :].astype(F32) * (FEAT**-0.5)
        query = query_f32.astype(BF16)
        query_rows = jnp.transpose(query_f32).astype(BF16)
        start_row = start_ref[:, ti * GROUP : (ti + 1) * GROUP]
        inverse = 1.0 / denom_ref[ti]
        cot = cot_ref[ti].astype(F32)
        cot_denom = -jnp.sum(cot * numer_ref[ti], axis=0, keepdims=True) * (inverse * inverse)
        cot_f32 = cot * inverse
        cot_numer = cot_f32.astype(BF16)
        cot_rows = jnp.transpose(cot_f32).astype(BF16)
        query_sum = jnp.zeros((FEAT, GROUP), F32)
        for si in range(ti + 1):
            one = nn(keys[si], query) + 1.0
            mask = pair_mask(start_row, si, ti, 0, GROUP)
            weight = jnp.where(mask, 0.5 * (one * one) + 0.5, 0.0).astype(BF16)
            value_sum[si] += nn(weight, cot_rows)
            cot_weight = nn(values[si], cot_numer) + cot_denom
            cot_score = jnp.where(mask, cot_weight * one, 0.0).astype(BF16)
            key_sum[si] += nn(cot_score, query_rows)
            query_sum = query_sum + nn(qkv_ref[si, FEAT : 2 * FEAT, :], cot_score)
        out_ref[ti, 0:FEAT, :] = (query_sum * (FEAT**-0.5)).astype(BF16)
    for si in range(4):
        out_ref[si, FEAT : 2 * FEAT, :] = jnp.transpose(key_sum[si]).astype(BF16)
        out_ref[si, 2 * FEAT :, :] = jnp.transpose(value_sum[si]).astype(BF16)
    for d, ref in enumerate((g0, g1, g2, g3)):
        ref[...] = out_ref[(at_ref[2] + d) % 4]


def attention_backward(order, at, qkv, cot, numer, denom, start_row, wait):
    return order.call(
        backward_kernel,
        "attention_backward",
        (like(HEAD_ROWS, GROUP),) * 4,
        (at, *cot, qkv, numer, denom, start_row),
        [
            pltpu.VMEM((4, HEAD_ROWS, GROUP), BF16),
            pltpu.VMEM((4, HEAD_V, GROUP), BF16),
            pltpu.VMEM((4, GROUP, FEAT), BF16),
            pltpu.VMEM((4, GROUP, HEAD_V), BF16),
            pltpu.VMEM((4, GROUP, FEAT), F32),
            pltpu.VMEM((4, GROUP, HEAD_V), F32),
        ],
        wait,
        in_specs=[SMEM] + [WHOLE] * 8,
        out_specs=(WHOLE,) * 4,
    )


VMEM_LIMIT = 52 * 2**20


class Order:
    def __init__(self):
        self.last = ()

    def call(self, kernel, name, out_shape, args, scratch=(), wait=(), **specs):
        at, first, *rest = args
        first = lax.optimization_barrier((first, *self.last, *wait))[0]
        if "grid_spec" not in specs:
            specs["scratch_shapes"] = list(scratch)
        out = pl.pallas_call(
            kernel,
            out_shape=out_shape,
            compiler_params=pltpu.CompilerParams(vmem_limit_bytes=VMEM_LIMIT),
            cost_estimate=pl.CostEstimate(flops=1, bytes_accessed=1, transcendentals=0),
            name=name,
            **specs,
        )(at, first, *rest)
        self.last = (out[0] if isinstance(out, (tuple, list)) else out,)
        return out


SMEM = pl.BlockSpec(memory_space=pltpu.SMEM)
WHOLE = pl.BlockSpec(memory_space=pltpu.VMEM)


def spec(*shape, at=None):
    def index(i):
        return tuple(i if k == at else 0 for k in range(len(shape)))

    return pl.BlockSpec(shape, index)


def like(*shape, dtype=BF16):
    return jax.ShapeDtypeStruct(shape, dtype)


def piece_at(at_ref, place, own_core):
    core = at_ref[1] if own_core else 1 - at_ref[1]
    return pl.multiple_of(((at_ref[0] + place) % 4 * 2 + core) * PIECE, PIECE)


def inverse_rms(rows):
    return lax.rsqrt(jnp.mean(rows * rows, axis=1, keepdims=True) + EPS)


def norm_back(grad_normed, unit, inverse, gains):
    scaled = grad_normed * gains
    return inverse * (scaled - unit * jnp.mean(scaled * unit, axis=1, keepdims=True))


RING_ROWS = ((0, 0, TOK), (1, 0, TOK), (2, 0, TOK // 2), (2, TOK // 2, TOK // 2), (3, 0, TOK))


HALF_ROWS = (HEAD_ROWS + HEAD_V // 2) // 2


def project_kernel(at_ref, *refs):
    tokens, weights, gain_ref = refs[:5], refs[5:10], refs[10]
    outs, normed_ref = refs[11:15], refs[15]
    for token_ref, (d, first, count) in zip(tokens, RING_ROWS):
        rows = token_ref[...].astype(F32)
        normed = (rows * inverse_rms(rows) * gain_ref[...]).astype(BF16)
        at = pl.multiple_of((at_ref[3] + d) % 4 * TOK, TOK) + first
        normed_ref[pl.ds(pl.multiple_of(at, count), count), :] = normed
    normed = normed_ref[...]
    for d, w_ref in ((0, weights[0]), (1, weights[1]), (3, weights[4])):
        outs[d][...] = nt(w_ref[:HEAD_ROWS, :], normed).astype(BF16)
    outs[2][:HALF_ROWS, :] = nt(weights[2][...], normed).astype(BF16)
    outs[2][HALF_ROWS:, :] = nt(weights[3][: HEAD_ROWS - HALF_ROWS, :], normed).astype(BF16)


def project(order, at, token_blocks, head_blocks, gain, wait):
    return order.call(
        project_kernel,
        "project",
        (like(HEAD_ROWS, GROUP),) * 4 + (like(GROUP, D),),
        (at, *token_blocks, *head_blocks, gain[None, :]),
        wait=wait,
        in_specs=[SMEM] + [WHOLE] * 11,
        out_specs=(WHOLE,) * 5,
    )


def half_at(at_ref, own):
    core = at_ref[1] if own else 1 - at_ref[1]
    return pl.ds(pl.multiple_of(core * 1024, 1024), 1024)


RING_LIKE = tuple(like(count, D) for _, _, count in RING_ROWS)


def at_place(at_ref, d):
    return pl.ds(pl.multiple_of((at_ref[3] + d) % 4 * TOK, TOK), TOK)


def out_kernel(at_ref, m0, m1, m2, m3, own_ref, other_ref, *refs):
    outs, (mixed, rows, weights) = refs[:5], refs[5:]
    for d, mixed_ref in enumerate((m0, m3, m2, m1)):
        mixed[:, d * HEAD_V : (d + 1) * HEAD_V] = jnp.transpose(mixed_ref[...].astype(F32)).astype(
            BF16
        )
        head_weights(at_ref, own_ref, other_ref, weights, d)
    rows[...] = nn(mixed[...], weights[...]).astype(BF16)
    for out_ref, (d, first, count) in zip(outs, RING_ROWS):
        at = pl.multiple_of((at_ref[3] + d) % 4 * TOK + first, count)
        out_ref[...] = rows[pl.ds(at, count), :]


def head_weights(at_ref, own_ref, other_ref, weights, d):
    half = HEAD_V // 2
    for core, w_ref in ((at_ref[1], own_ref), (1 - at_ref[1], other_ref)):
        first = pl.multiple_of(d * HEAD_V + core * half, half)
        weights[pl.ds(first, half), :] = w_ref[d]


def out_projection(order, at, mixed, weights, wait):
    return order.call(
        out_kernel,
        "out_projection",
        RING_LIKE,
        (at, *mixed, *weights),
        [
            pltpu.VMEM((GROUP, GROUP), BF16),
            pltpu.VMEM((GROUP, D), BF16),
            pltpu.VMEM((GROUP, D), BF16),
        ],
        wait,
        in_specs=[SMEM] + [WHOLE] * 6,
        out_specs=(WHOLE,) * 5,
    )


def middle_kernel(at_ref, p0, p1, p3, token_ref, gain_ref, mid_ref, normed_ref):
    branch = p0[...].astype(F32) + p1[...].astype(F32) + p3[...].astype(F32)
    mid = token_ref[...].astype(F32) + branch
    mid_ref[...] = mid
    normed_ref[...] = (mid * inverse_rms(mid) * gain_ref[...]).astype(BF16)


def middle(order, at, parts, tokens, gain, wait):
    return order.call(
        middle_kernel,
        "middle",
        (like(TOK, D, dtype=F32), like(TOK, D)),
        (at, *parts, tokens, gain[None, :]),
        wait=wait,
        in_specs=[SMEM] + [WHOLE] * 5,
        out_specs=(WHOLE, WHOLE),
    )


RING = ((0, TOK), (TOK, TOK), (2 * TOK, TOK // 2), (2 * TOK + TOK // 2, TOK // 2), (3 * TOK, TOK))
RING_SPECS = [spec(count, D) for _, count in RING]


def feed_kernel(at_ref, *refs):
    blocks, cot_refs, weight_refs = refs[:5], refs[5:10], refs[10:12]
    (hidden_ref, gate_ref, up_ref), outs = refs[12:15], refs[15:20]
    rows, cots, weights, downs, total, gate_up_sems, down_sems = refs[20:]

    def gate_up_copy(z, own):
        return pltpu.make_async_copy(
            weight_refs[own].at[z, pl.ds(0, 2 * HID)], weights.at[z, own], gate_up_sems.at[z, own]
        )

    def down_copy(z, own):
        return pltpu.make_async_copy(
            weight_refs[own].at[z, pl.ds(2 * HID, HID)],
            downs.at[z, :, pl.ds(own * 1024, 1024)],
            down_sems.at[z, own],
        )

    for z in range(4):
        for own in (0, 1):
            gate_up_copy(z, own).start()
            down_copy(z, own).start()
    for (first, count), block, cot_ref in zip(RING, blocks, cot_refs):
        at = slice(first, first + count)
        for own in (0, 1):
            rows[own, at, :] = block[:, half_at(at_ref, own == 0)]
            cots[at, own * 1024 : (own + 1) * 1024] = cot_ref[:, half_at(at_ref, own == 0)]
    for z in range(4):
        for own in (0, 1):
            gate_up_copy(z, own).wait()
            down_copy(z, own).wait()
        both_rows = nt(weights[z, 0], rows[0]) + nt(weights[z, 1], rows[1])
        gate_rows, up_rows = both_rows[:HID], both_rows[HID:]
        grad_hidden = nt(downs[z], cots[...])
        sigmoid_gate = 1.0 / (1.0 + jnp.exp(-gate_rows))
        silu_gate = gate_rows * sigmoid_gate
        hidden_ref[z] = (silu_gate * up_rows).astype(BF16)
        up_delta = (grad_hidden * silu_gate).astype(BF16)
        gate_delta = (
            grad_hidden * up_rows * (sigmoid_gate + silu_gate * (1.0 - sigmoid_gate))
        ).astype(BF16)
        gate_ref[z] = gate_delta
        up_ref[z] = up_delta
        both_delta = jnp.concatenate([gate_delta, up_delta], axis=0)
        for own in (0, 1):
            part = tn(both_delta, weights[z, own])
            if z == 0:
                total[own] = part
            elif z < 3:
                total[own] += part
            else:
                part = (part + total[own]).astype(BF16)
                for (first, count), out_ref in zip(RING, outs):
                    out_ref[:, half_at(at_ref, own == 0)] = part[first : first + count]


def feed(order, at, second_blocks, cot_blocks, weights):
    deltas = like(4, HID, GROUP)
    return order.call(
        feed_kernel,
        "feed",
        (deltas, deltas, deltas) + RING_LIKE,
        (at, *second_blocks, *cot_blocks, *weights),
        [
            pltpu.VMEM((2, GROUP, 1024), BF16),
            pltpu.VMEM((GROUP, D), BF16),
            pltpu.VMEM((4, 2, 2 * HID, 1024), BF16),
            pltpu.VMEM((4, HID, D), BF16),
            pltpu.VMEM((2, GROUP, 1024), F32),
            pltpu.SemaphoreType.DMA((4, 2)),
            pltpu.SemaphoreType.DMA((4, 2)),
        ],
        in_specs=[SMEM] + [WHOLE] * 10 + [pl.BlockSpec(memory_space=pl.ANY)] * 2,
        out_specs=(WHOLE,) * 8,
    )


def down_kernel(at_ref, hidden_ref, own_ref, other_ref, *refs):
    out_ref, rows, downs, sems = refs

    def copy(own):
        weight_ref = own_ref if own == 0 else other_ref
        return pltpu.make_async_copy(
            weight_ref.at[:, pl.ds(2 * HID, HID)], downs.at[own], sems.at[own]
        )

    copy(0).start()
    copy(1).start()
    for z in range(4):
        rows[z] = jnp.transpose(hidden_ref[z].astype(F32)).astype(BF16)
    for own in (0, 1):
        copy(own).wait()
        part = nn(rows[0], downs[own, 0])
        for z in range(1, 4):
            part = part + nn(rows[z], downs[own, z])
        part = part.astype(BF16)
        for b in range(4):
            block = part[b * TOK : (b + 1) * TOK]
            out_ref[(at_ref[3] + b) % 4, :, half_at(at_ref, own == 0)] = block


def down(order, at, hidden, weights, wait):
    return order.call(
        down_kernel,
        "down",
        like(4, TOK, D),
        (at, hidden, *weights),
        [
            pltpu.VMEM((4, GROUP, HID), BF16),
            pltpu.VMEM((2, 4, HID, 1024), BF16),
            pltpu.SemaphoreType.DMA((2,)),
        ],
        wait,
        in_specs=[SMEM, WHOLE] + [pl.BlockSpec(memory_space=pl.ANY)] * 2,
        out_specs=WHOLE,
    )


def feed_grads_kernel(own, count, at_ref, *refs):
    lefts, blocks, rows = refs[:count], refs[count : count + 5], refs[-1]
    others, out_ref = refs[count + 5 : -2], refs[-2]
    step = pl.program_id(0)

    @pl.when(step == 0)
    def _():
        core = at_ref[1] if own else 1 - at_ref[1]
        for (first, size), block in zip(RING, blocks):
            for k in range(4):
                columns = pl.ds(pl.multiple_of((k * 2 + core) * PIECE, PIECE), PIECE)
                rows[first : first + size, k * PIECE : (k + 1) * PIECE] = block[:, columns]

    for i, left_ref in enumerate(lefts):
        part = nn(left_ref[0], rows[...])
        at = slice(i * HID, (i + 1) * HID)
        for k in range(4):
            block = part[:, k * PIECE : (k + 1) * PIECE]
            if own:
                block = block + others[0][k, 0, at, :].astype(F32)
            out_ref[k, 0, at, :] = block.astype(BF16)


def feed_grads(order, at, lefts, blocks, ahead, other=(), wait=()):
    own, count = bool(other), len(lefts)
    rows = count * HID

    def place(i, at_ref):
        return (i + 4 - at_ref[2]) % 4 if ahead else i

    grads = pl.BlockSpec((4, 1, rows, PIECE), lambda i, at_ref: (0, place(i, at_ref), 0, 0))
    return order.call(
        lambda *refs: feed_grads_kernel(own, count, *refs),
        "feed_grads_own" if own else "feed_grads",
        (like(4, 4, rows, PIECE),),
        (at, *lefts, *blocks, *other),
        wait=wait,
        grid_spec=pltpu.PrefetchScalarGridSpec(
            num_scalar_prefetch=1,
            grid=(4,),
            in_specs=[pl.BlockSpec((1, HID, GROUP), lambda i, at_ref: (i, 0, 0))] * count
            + [pl.BlockSpec((size, D), lambda i, at_ref: (0, 0)) for _, size in RING]
            + ([grads] if own else []),
            out_specs=(grads,),
            scratch_shapes=[pltpu.VMEM((GROUP, 1024), BF16)],
        ),
    )


def turn_kernel(
    at_ref, s0, s1, s3, mid_ref, cot_ref, gain_ref, branch_ref, grad_mid_ref, gain_part_ref
):
    grad_second = s0[...].astype(F32) + s1[...].astype(F32) + s3[...].astype(F32)
    mid = mid_ref[...]
    inverse = inverse_rms(mid)
    unit = mid * inverse
    gain_part_ref[...] = jnp.sum(grad_second * unit, axis=0, keepdims=True)
    grad_mid = cot_ref[...].astype(F32) + norm_back(grad_second, unit, inverse, gain_ref[...])
    grad_mid_ref[...] = grad_mid
    branch_ref[...] = grad_mid.astype(BF16)


def turn(order, at, second_sums, mid_rows, out_grad, gain):
    return order.call(
        turn_kernel,
        "turn",
        (like(TOK, D), like(TOK, D, dtype=F32), like(1, D, dtype=F32)),
        (at, *second_sums, mid_rows, out_grad, gain[None, :]),
        in_specs=[SMEM] + [WHOLE] * 6,
        out_specs=(WHOLE,) * 3,
    )


def back_kernel(at_ref, b0, b1, b2a, b2b, b3, own_ref, other_ref, *refs):
    outs, rows_ref, weights = refs[:4], refs[4], refs[5]
    for block_ref, (d, first, count) in zip((b0, b1, b2a, b2b, b3), RING_ROWS):
        at = pl.ds(pl.multiple_of((at_ref[3] + d) % 4 * TOK + first, count), count)
        rows_ref[at, :] = block_ref[...]
    for d in range(4):
        head_weights(at_ref, own_ref, other_ref, weights, d)
    total = nt(weights[...], rows_ref[...]).astype(BF16)
    for d, out_ref in enumerate(outs):
        out_ref[...] = total[d * HEAD_V : (d + 1) * HEAD_V, :]


def back_projection(order, at, branch_blocks, weights):
    return order.call(
        back_kernel,
        "back_projection",
        (like(HEAD_V, GROUP),) * 4 + (like(GROUP, D),),
        (at, *branch_blocks, *weights),
        [pltpu.VMEM((GROUP, D), BF16)],
        in_specs=[SMEM] + [WHOLE] * 7,
        out_specs=(WHOLE,) * 5,
    )


def own_first(at_ref, out, block, rows):
    for own in (0, 1):
        for k in range(4):
            columns = pl.ds(piece_at(at_ref, k, own == 0), PIECE)
            piece = own * 4 + k
            out[rows, piece * PIECE : (piece + 1) * PIECE] = block[:, columns]


def out_grads_kernel(at_ref, m0, m1, m2, m3, branch_ref, out_ref, rows):
    own_first(at_ref, rows, branch_ref, slice(0, GROUP))
    for back, mixed_ref in enumerate((m0, m1, m2, m3)):
        out_ref[(4 - back) % 4] = nn(mixed_ref[...], rows[...]).astype(BF16)


def out_grads(order, at, mixed, branch_rows):
    return order.call(
        out_grads_kernel,
        "out_grads",
        like(4, HEAD_V, D),
        (at, *mixed, branch_rows),
        [pltpu.VMEM((GROUP, D), BF16)],
        in_specs=[SMEM] + [WHOLE] * 5,
        out_specs=WHOLE,
    )


BOTH_ROWS = HEAD_V + HEAD_ROWS + 16


def head_grads_kernel(at_ref, *refs):
    (g0, g1, g2, g3), weights, normed_ref, gain_ref = refs[:4], refs[4:9], refs[9], refs[10]
    out_grad_ref, second_ref, own_ref, other_ref, rows = refs[11:]
    own_first(at_ref, rows, normed_ref, slice(0, GROUP))
    rest = HEAD_ROWS - HALF_ROWS
    places = (
        (g0, ((weights[0], HEAD_ROWS),)),
        (g3, ((weights[1], HEAD_ROWS),)),
        (g2, ((weights[2], HALF_ROWS), (weights[3], rest))),
        (g1, ((weights[4], HEAD_ROWS),)),
    )
    for own in (0, 1):
        sent_ref = own_ref if own == 0 else other_ref
        for k in range(4):
            columns = pl.ds(piece_at(at_ref, k, own == 0), PIECE)
            piece = slice((own * 4 + k) * PIECE, (own * 4 + k + 1) * PIECE)
            gain_part = jnp.zeros((1, PIECE), F32)
            for d, (grads_ref, w_refs) in enumerate(places):
                part = nn(grads_ref[...], rows[:, piece])
                first = 0
                for w_ref, count in w_refs:
                    weighted = part[first : first + count] * w_ref[:count, columns].astype(F32)
                    gain_part = gain_part + jnp.sum(weighted, axis=0, keepdims=True)
                    first += count
                sent_ref[d, k, :HEAD_V] = out_grad_ref[d, :, piece]
                sent_ref[d, k, HEAD_V : HEAD_V + HEAD_ROWS] = part.astype(BF16)
            gain_part = gain_part / gain_ref[:, columns]
            gain_rows = jnp.where(
                lax.broadcasted_iota(jnp.int32, (16, PIECE), 0) == 0,
                gain_part,
                second_ref[:, columns],
            ).astype(BF16)
            for d in range(4):
                sent_ref[d, k, HEAD_V + HEAD_ROWS :] = gain_rows


def head_grads(order, at, grads, head_blocks, normed, gain, out_part, second_part, wait):
    both = like(4, 4, BOTH_ROWS, PIECE)
    return order.call(
        head_grads_kernel,
        "head_grads",
        (both, both),
        (at, *grads, *head_blocks, normed, gain[None, :], out_part, second_part),
        [pltpu.VMEM((GROUP, D), BF16)],
        wait,
        in_specs=[SMEM] + [WHOLE] * 13,
        out_specs=(WHOLE,) * 2,
    )


def add_kernel(at_ref, mine_ref, other_ref, *outs):
    for d, out_ref in enumerate(outs):
        out_ref[...] = (mine_ref[d].astype(F32) + other_ref[d].astype(F32)).astype(BF16)


def add_blocks(order, at, mine, other):
    return order.call(
        add_kernel,
        "add_blocks",
        (like(4, BOTH_ROWS, PIECE),) * 4,
        (at, mine, other),
        in_specs=[SMEM] + [WHOLE] * 2,
        out_specs=(WHOLE,) * 4,
    )


def first_kernel(at_ref, *refs):
    grads, (w0, w1, w2a, w2b, w3), outs = refs[:4], refs[4:9], refs[9:14]
    rest = HEAD_ROWS - HALF_ROWS
    for d in range(4):
        columns = at_place(at_ref, d)
        part = tn(grads[0][:, columns], w0[:HEAD_ROWS, :])
        part = part + tn(grads[3][:, columns], w1[:HEAD_ROWS, :])
        part = part + tn(grads[1][:, columns], w3[:HEAD_ROWS, :])
        part = part + tn(grads[2][:HALF_ROWS, columns], w2a[...])
        part = (part + tn(grads[2][HALF_ROWS:, columns], w2b[:rest, :])).astype(BF16)
        for out_ref, (place, first, count) in zip(outs, RING_ROWS):
            if place == d:
                out_ref[...] = part[first : first + count]


def first_part(order, at, grads, head_blocks, wait):
    return order.call(
        first_kernel,
        "first_part",
        RING_LIKE,
        (at, *grads, *head_blocks),
        wait=wait,
        in_specs=[SMEM] + [WHOLE] * 9,
        out_specs=(WHOLE,) * 5,
    )


def collect_kernel(turned, at_ref, *refs):
    outs = refs[5:]
    for own in (True, False):
        for d in range(4):
            columns = pl.ds(piece_at(at_ref, d, own), PIECE)
            first = 0
            for i, out_ref in enumerate(outs):
                rows = out_ref.shape[1 if i == turned else 0]
                at = slice(first, first - (-rows // 16 * 16))
                block = (refs[d][at, :] if own else refs[4][d, at, :]).astype(F32)[:rows]
                if i == turned:
                    out_ref[columns, :] = jnp.transpose(block)
                else:
                    out_ref[:, columns] = block
                first += -rows // 16 * -16


def collect(order, at, mine, name, *rows, turned=None):
    other = swapped(jnp.stack(mine))
    return order.call(
        lambda *refs: collect_kernel(turned, *refs),
        name,
        tuple(
            like(D, r, dtype=F32) if i == turned else like(r, D, dtype=F32)
            for i, r in enumerate(rows)
        ),
        (at, *mine, other),
        in_specs=[SMEM] + [WHOLE] * 5,
        out_specs=(WHOLE,) * len(rows),
    )


def after(array, *needed):
    return lax.optimization_barrier((array, *needed))[0]


def body(
    tokens,
    doc_start,
    gain_first,
    w_query,
    w_key,
    w_value,
    w_out,
    gain_second,
    w_gate,
    w_up,
    w_down,
    out_grad,
):
    order = Order()
    at = jnp.stack([lax.axis_index(a) for a in AXES]).astype(jnp.int32)
    x_at, core, z_at, y_at = (at[i] for i in range(4))

    token_blocks = ring_gathered(tokens, "y")
    out_half = lax.dynamic_slice_in_dim(w_out, core * (HEAD_V // 2), HEAD_V // 2, 0)
    w_head = jnp.concatenate([w_query.T, w_key.T, w_value.T, out_half], axis=0)
    head_blocks = ring_gathered(w_head, "z")
    feed_half = jnp.concatenate([w_gate.T, w_up.T, w_down], axis=0)
    feed_half = lax.dynamic_slice_in_dim(feed_half, core * 1024, 1024, 1)
    *qkv, group_normed = project(order, at, token_blocks, head_blocks, gain_first, ())
    feed_mine = lax.all_gather(after(feed_half, group_normed), "z", axis=0)
    qkv = exchanged(qkv, "z")
    out_mine = jnp.stack([block[-(HEAD_V // 2) :] for block in (*head_blocks[:2], *head_blocks[3:])])
    out_mine = after(out_mine, *qkv)
    out_weights = (out_mine, swapped(out_mine))
    cot_blocks = gathered(after(out_grad, *qkv), "y")

    positions = jnp.arange(SEQ, dtype=jnp.int32)
    start_row = lax.cummax(jnp.where(doc_start != 0, positions, 0))[None, :]
    *mixed, numer, denom, qkv = attention_forward(order, at, qkv, start_row, ())
    mixed = exchanged(mixed, "z")
    p0, p1, *p2, p3 = out_projection(order, at, mixed, out_weights, ())
    parts = (p0, *ring_end(ring_start(p2, "y"), p1, p3, "y"))
    mid_rows, second_normed = middle(order, at, parts, tokens, gain_second, cot_blocks)

    cot_blocks = [*cot_blocks[:2], cot_blocks[2][:64], cot_blocks[2][64:], cot_blocks[3]]
    second_blocks = ring_gathered(second_normed, "y")
    feed_mine = after(feed_mine, second_blocks[1], second_blocks[4])
    feed_weights = (feed_mine, swapped(feed_mine))
    hidden, gate_delta, up_delta, s0, s1, *s2, s3 = feed(
        order, at, second_blocks, cot_blocks, feed_weights
    )
    arrived = ring_start(s2, "y")
    second_sums = (s0, *ring_end(arrived, s1, s3, "y"))
    deltas = (gate_delta, up_delta)
    (gu_grads,) = feed_grads(order, at, deltas, second_blocks, False, wait=arrived)
    gu_grads = swapped(gu_grads)
    (down_grads,) = feed_grads(order, at, (hidden,), cot_blocks, True)
    down_grads = swapped(down_grads)

    grad_branch, grad_mid, gain_second_part = turn(
        order, at, second_sums, mid_rows, out_grad, gain_second
    )
    branch_blocks = ring_gathered(grad_branch, "y")
    (gu_grads,) = feed_grads(
        order,
        at,
        deltas,
        second_blocks,
        False,
        (gu_grads,),
        wait=(branch_blocks[1], branch_blocks[4]),
    )
    gu_sum = lax.psum_scatter(
        gu_grads.reshape(16, 2 * HID, PIECE), ("x", "z"), scatter_dimension=0
    )
    b_parts = down(order, at, hidden, feed_weights, ())
    *grad_mixed, branch_rows = back_projection(order, at, branch_blocks, out_weights)
    grad_mixed = exchanged(grad_mixed, "z")
    b_parts = lax.all_to_all(after(b_parts, branch_rows), "y", 0, 0)
    (down_grads,) = feed_grads(order, at, (hidden,), cot_blocks, True, (down_grads,))
    out_part = out_grads(order, at, mixed, branch_rows)
    grads = attention_backward(order, at, qkv, grad_mixed, numer, denom, start_row, ())
    grads = exchanged(grads, "z")

    def added(blocks):
        total = (blocks[0].astype(F32) + blocks[1].astype(F32)) + (
            blocks[2].astype(F32) + blocks[3].astype(F32)
        )
        return total.astype(BF16)

    mine, other = head_grads(
        order,
        at,
        grads,
        head_blocks,
        group_normed,
        gain_first,
        out_part,
        gain_second_part,
        (b_parts,),
    )
    down_grads = lax.all_to_all(after(down_grads, b_parts), "x", 0, 0)
    other = swapped(other)
    f0, f1, *f2, f3 = first_part(order, at, grads, head_blocks, ())
    head_part = added(exchanged(add_blocks(order, at, mine, other), "z"))
    from_back, from_ahead = ring_end(ring_start(f2, "y"), f1, f3, "y")
    head_sum = added(exchanged([head_part[d] for d in range(4)], "x"))
    down_part = jnp.sum(after(down_grads, head_part).astype(F32), axis=0).astype(BF16)
    down_sum = added(exchanged([down_part[d] for d in range(4)], "z"))
    grad_first = f0.astype(F32) + from_back.astype(F32) + from_ahead.astype(F32)
    block_out = mid_rows + jnp.sum(b_parts.astype(F32), axis=0)
    x_rows = tokens.astype(F32)
    first_inv = inverse_rms(x_rows)
    input_grad = grad_mid + norm_back(grad_first, x_rows * first_inv, first_inv, gain_first)

    grad_out, grad_query, grad_key, grad_value, gains = collect(
        order,
        at,
        gathered(head_sum, "x"),
        "collect_heads",
        HEAD_V,
        FEAT,
        FEAT,
        HEAD_V,
        2,
        turned=3,
    )
    gains = gathered(gains, "y")
    gains = (gains[0] + gains[1]) + (gains[2] + gains[3])
    ffn_sum = jnp.concatenate([gu_sum, down_sum], axis=0)
    grad_gate, grad_up, grad_down = collect(
        order, at, gathered(ffn_sum, "x"), "collect_feed", HID, HID, HID
    )
    return (
        block_out,
        input_grad,
        gains[0],
        grad_query.T,
        grad_key.T,
        grad_value,
        grad_out,
        gains[1],
        grad_gate.T,
        grad_up.T,
        grad_down,
    )


def solution(mesh):
    fine = Mesh(mesh.devices.reshape(4, 2, 4, 4), AXES)
    rows, dp, mp = P(AXES, None), P(("x", "core")), ("z", "y")
    return jax.shard_map(
        body,
        mesh=fine,
        in_specs=(
            rows,
            dp,
            P(),
            P(None, mp),
            P(None, mp),
            P(None, mp),
            P(mp, None),
            P(),
            P(None, mp),
            P(None, mp),
            P(mp, None),
            rows,
        ),
        out_specs=(
            rows,
            rows,
            P(),
            P(None, mp),
            P(None, mp),
            P(None, mp),
            P(mp, None),
            P(),
            P(None, mp),
            P(None, mp),
            P(mp, None),
        ),
        check_vma=False,
    )
```

```python
import jax
import jax.numpy as jnp
from jax import lax
from jax.experimental import pallas as pl
from jax.experimental.pallas import tpu as pltpu
from jax.sharding import Mesh, PartitionSpec as P

FEAT = 16
HEAD_V = 128
EPS = 1e-05
F32 = jnp.float32
BF16 = jnp.bfloat16
TOK = 128
GROUP = 512
SEQ = 2048
HEAD_ROWS = 2 * FEAT + HEAD_V
AXES = ("x", "core", "z", "y")
D = 2048
HID = 352
PIECE = 256


def shifted(array, axis, by):
    return lax.ppermute(array, axis, [(i, (i + by) % 4) for i in range(4)])


def swapped(array):
    return lax.ppermute(array, "core", [(0, 1), (1, 0)])


def swapped_each(arrays):
    return [swapped(array) for array in arrays]


def gathered(array, axis):
    return [
        array,
        shifted(array, axis, 3),
        shifted(array, axis, 2),
        shifted(array, axis, 1),
    ]


def ring_gathered(array, axis):
    half = array.shape[0] // 2
    ahead, back = shifted(array, axis, 3), shifted(array, axis, 1)
    return [array, ahead, shifted(back[:half], axis, 1), shifted(ahead[half:], axis, 3), back]


def ring_start(opposite, axis):
    return shifted(opposite[0], axis, 1), shifted(opposite[1], axis, 3)


def ring_end(arrived, ahead, back, axis):
    half = ahead.shape[0] // 2
    first, second = arrived
    ahead = jnp.concatenate([ahead[:half] + first, ahead[half:]], axis=0)
    back = jnp.concatenate([back[:half], back[half:] + second], axis=0)
    return shifted(ahead, axis, 1), shifted(back, axis, 3)


def exchanged(blocks, axis):
    return [
        blocks[0],
        shifted(blocks[1], axis, 1),
        shifted(blocks[2], axis, 2),
        shifted(blocks[3], axis, 3),
    ]


def in_order(blocks, at):
    stacked = jnp.stack(blocks)
    return jnp.concatenate(
        [lax.dynamic_index_in_dim(stacked, (j - at) % 4, 0, keepdims=False) for j in range(4)], axis=0
    )


def nn(left, right):
    return jnp.dot(left, right, preferred_element_type=F32)


def nt(left, right):
    return lax.dot_general(left, right, (((1,), (1,)), ((), ())), preferred_element_type=F32)


def tn(left, right):
    return lax.dot_general(left, right, (((0,), (0,)), ((), ())), preferred_element_type=F32)


def pair_mask(start_row, si, ti, first, rows):
    row = lax.broadcasted_iota(jnp.int32, (rows, GROUP), 0) + (si * GROUP + first)
    mask = row >= start_row
    if si == ti:
        column = lax.broadcasted_iota(jnp.int32, (rows, GROUP), 1) + ti * GROUP
        mask = mask & (row <= column)
    return mask


def forward_kernel(
    at_ref,
    q0,
    q1,
    q2,
    q3,
    start_ref,
    m0,
    m1,
    m2,
    m3,
    numer_ref,
    denom_ref,
    qkv_ref,
    mixed_ref,
    keys,
):
    for d, ref in enumerate((q0, q1, q2, q3)):
        qkv_ref[(at_ref[2] + 4 - d) % 4] = ref[...]
    for si in range(4):
        keys[si] = jnp.transpose(qkv_ref[si, FEAT : 2 * FEAT, :].astype(F32)).astype(BF16)
    for ti in range(4):
        query = (qkv_ref[ti, 0:FEAT, :].astype(F32) * (FEAT**-0.5)).astype(BF16)
        start_row = start_ref[:, ti * GROUP : (ti + 1) * GROUP]
        numer = jnp.zeros((HEAD_V, GROUP), F32)
        denom = jnp.zeros((1, GROUP), F32)
        for si in range(ti + 1):
            one = nn(keys[si], query) + 1.0
            weight = jnp.where(
                pair_mask(start_row, si, ti, 0, GROUP), 0.5 * (one * one) + 0.5, 0.0
            )
            denom = denom + jnp.sum(weight, axis=0, keepdims=True)
            numer = numer + nn(qkv_ref[si, 2 * FEAT :, :], weight.astype(BF16))
        numer_ref[ti] = numer
        denom_ref[ti] = denom
        mixed_ref[ti] = (numer / denom).astype(BF16)
    for d, ref in enumerate((m0, m1, m2, m3)):
        ref[...] = mixed_ref[(at_ref[2] + d) % 4]


def attention_forward(order, at, qkv, start_row, wait):
    return order.call(
        forward_kernel,
        "attention_forward",
        (like(HEAD_V, GROUP),) * 4
        + (
            like(4, HEAD_V, GROUP, dtype=F32),
            like(4, 1, GROUP, dtype=F32),
            like(4, HEAD_ROWS, GROUP),
        ),
        (at, *qkv, start_row),
        [pltpu.VMEM((4, HEAD_V, GROUP), BF16), pltpu.VMEM((4, GROUP, FEAT), BF16)],
        wait,
        in_specs=[SMEM] + [WHOLE] * 5,
        out_specs=(WHOLE,) * 7,
    )


def backward_kernel(
    at_ref,
    c0,
    c1,
    c2,
    c3,
    qkv_ref,
    numer_ref,
    denom_ref,
    start_ref,
    g0,
    g1,
    g2,
    g3,
    out_ref,
    cot_ref,
    keys,
    values,
    key_sum,
    value_sum,
):
    for d, ref in enumerate((c0, c1, c2, c3)):
        cot_ref[(at_ref[2] + 4 - d) % 4] = ref[...]
    for si in range(4):
        keys[si] = jnp.transpose(qkv_ref[si, FEAT : 2 * FEAT, :].astype(F32)).astype(BF16)
        values[si] = jnp.transpose(qkv_ref[si, 2 * FEAT :, :].astype(F32)).astype(BF16)
    key_sum[...] = jnp.zeros_like(key_sum)
    value_sum[...] = jnp.zeros_like(value_sum)
    for ti in range(4):
        query_f32 = qkv_ref[ti, 0:FEAT, :].astype(F32) * (FEAT**-0.5)
        query = query_f32.astype(BF16)
        query_rows = jnp.transpose(query_f32).astype(BF16)
        start_row = start_ref[:, ti * GROUP : (ti + 1) * GROUP]
        inverse = 1.0 / denom_ref[ti]
        cot = cot_ref[ti].astype(F32)
        cot_denom = -jnp.sum(cot * numer_ref[ti], axis=0, keepdims=True) * (inverse * inverse)
        cot_f32 = cot * inverse
        cot_numer = cot_f32.astype(BF16)
        cot_rows = jnp.transpose(cot_f32).astype(BF16)
        query_sum = jnp.zeros((FEAT, GROUP), F32)
        for si in range(ti + 1):
            one = nn(keys[si], query) + 1.0
            mask = pair_mask(start_row, si, ti, 0, GROUP)
            weight = jnp.where(mask, 0.5 * (one * one) + 0.5, 0.0).astype(BF16)
            value_sum[si] += nn(weight, cot_rows)
            cot_weight = nn(values[si], cot_numer) + cot_denom
            cot_score = jnp.where(mask, cot_weight * one, 0.0).astype(BF16)
            key_sum[si] += nn(cot_score, query_rows)
            query_sum = query_sum + nn(qkv_ref[si, FEAT : 2 * FEAT, :], cot_score)
        out_ref[ti, 0:FEAT, :] = (query_sum * (FEAT**-0.5)).astype(BF16)
    for si in range(4):
        out_ref[si, FEAT : 2 * FEAT, :] = jnp.transpose(key_sum[si]).astype(BF16)
        out_ref[si, 2 * FEAT :, :] = jnp.transpose(value_sum[si]).astype(BF16)
    for d, ref in enumerate((g0, g1, g2, g3)):
        ref[...] = out_ref[(at_ref[2] + d) % 4]


def attention_backward(order, at, qkv, cot, numer, denom, start_row, wait):
    return order.call(
        backward_kernel,
        "attention_backward",
        (like(HEAD_ROWS, GROUP),) * 4,
        (at, *cot, qkv, numer, denom, start_row),
        [
            pltpu.VMEM((4, HEAD_ROWS, GROUP), BF16),
            pltpu.VMEM((4, HEAD_V, GROUP), BF16),
            pltpu.VMEM((4, GROUP, FEAT), BF16),
            pltpu.VMEM((4, GROUP, HEAD_V), BF16),
            pltpu.VMEM((4, GROUP, FEAT), F32),
            pltpu.VMEM((4, GROUP, HEAD_V), F32),
        ],
        wait,
        in_specs=[SMEM] + [WHOLE] * 8,
        out_specs=(WHOLE,) * 4,
    )


VMEM_LIMIT = 52 * 2**20


class Order:
    def __init__(self):
        self.last = ()

    def call(self, kernel, name, out_shape, args, scratch=(), wait=(), **specs):
        at, first, *rest = args
        first = lax.optimization_barrier((first, *self.last, *wait))[0]
        if "grid_spec" not in specs:
            specs["scratch_shapes"] = list(scratch)
        out = pl.pallas_call(
            kernel,
            out_shape=out_shape,
            compiler_params=pltpu.CompilerParams(vmem_limit_bytes=VMEM_LIMIT),
            cost_estimate=pl.CostEstimate(flops=1, bytes_accessed=1, transcendentals=0),
            name=name,
            **specs,
        )(at, first, *rest)
        self.last = (out[0] if isinstance(out, (tuple, list)) else out,)
        return out


SMEM = pl.BlockSpec(memory_space=pltpu.SMEM)
WHOLE = pl.BlockSpec(memory_space=pltpu.VMEM)


def spec(*shape, at=None):
    def index(i):
        return tuple(i if k == at else 0 for k in range(len(shape)))

    return pl.BlockSpec(shape, index)


def like(*shape, dtype=BF16):
    return jax.ShapeDtypeStruct(shape, dtype)


def piece_at(at_ref, place, own_core):
    core = at_ref[1] if own_core else 1 - at_ref[1]
    return pl.multiple_of(((at_ref[0] + place) % 4 * 2 + core) * PIECE, PIECE)


def inverse_rms(rows):
    return lax.rsqrt(jnp.mean(rows * rows, axis=1, keepdims=True) + EPS)


def norm_back(grad_normed, unit, inverse, gains):
    scaled = grad_normed * gains
    return inverse * (scaled - unit * jnp.mean(scaled * unit, axis=1, keepdims=True))


RING_ROWS = ((0, 0, TOK), (1, 0, TOK), (2, 0, TOK // 2), (2, TOK // 2, TOK // 2), (3, 0, TOK))


HALF_ROWS = (HEAD_ROWS + HEAD_V // 2) // 2


def project_kernel(at_ref, *refs):
    tokens, weights, gain_ref = refs[:5], refs[5:10], refs[10]
    outs, normed_ref = refs[11:15], refs[15]
    for token_ref, (d, first, count) in zip(tokens, RING_ROWS):
        rows = token_ref[...].astype(F32)
        normed = (rows * inverse_rms(rows) * gain_ref[...]).astype(BF16)
        at = pl.multiple_of((at_ref[3] + d) % 4 * TOK, TOK) + first
        normed_ref[pl.ds(pl.multiple_of(at, count), count), :] = normed
    normed = normed_ref[...]
    for d, w_ref in ((0, weights[0]), (1, weights[1]), (3, weights[4])):
        outs[d][...] = nt(w_ref[:HEAD_ROWS, :], normed).astype(BF16)
    outs[2][:HALF_ROWS, :] = nt(weights[2][...], normed).astype(BF16)
    outs[2][HALF_ROWS:, :] = nt(weights[3][: HEAD_ROWS - HALF_ROWS, :], normed).astype(BF16)


def project(order, at, token_blocks, head_blocks, gain, wait):
    return order.call(
        project_kernel,
        "project",
        (like(HEAD_ROWS, GROUP),) * 4 + (like(GROUP, D),),
        (at, *token_blocks, *head_blocks, gain[None, :]),
        wait=wait,
        in_specs=[SMEM] + [WHOLE] * 11,
        out_specs=(WHOLE,) * 5,
    )


def half_at(at_ref, own):
    core = at_ref[1] if own else 1 - at_ref[1]
    return pl.ds(pl.multiple_of(core * 1024, 1024), 1024)


RING_LIKE = tuple(like(count, D) for _, _, count in RING_ROWS)


def at_place(at_ref, d):
    return pl.ds(pl.multiple_of((at_ref[3] + d) % 4 * TOK, TOK), TOK)


def out_kernel(at_ref, m0, m1, m2, m3, own_ref, other_ref, *refs):
    outs, (mixed, rows, weights) = refs[:5], refs[5:]
    for d, mixed_ref in enumerate((m0, m3, m2, m1)):
        mixed[:, d * HEAD_V : (d + 1) * HEAD_V] = jnp.transpose(mixed_ref[...].astype(F32)).astype(
            BF16
        )
        head_weights(at_ref, own_ref, other_ref, weights, d)
    rows[...] = nn(mixed[...], weights[...]).astype(BF16)
    for out_ref, (d, first, count) in zip(outs, RING_ROWS):
        at = pl.multiple_of((at_ref[3] + d) % 4 * TOK + first, count)
        out_ref[...] = rows[pl.ds(at, count), :]


def head_weights(at_ref, own_ref, other_ref, weights, d):
    half = HEAD_V // 2
    for core, w_ref in ((at_ref[1], own_ref), (1 - at_ref[1], other_ref)):
        first = pl.multiple_of(d * HEAD_V + core * half, half)
        weights[pl.ds(first, half), :] = w_ref[d]


def out_projection(order, at, mixed, weights, wait):
    return order.call(
        out_kernel,
        "out_projection",
        RING_LIKE,
        (at, *mixed, *weights),
        [
            pltpu.VMEM((GROUP, GROUP), BF16),
            pltpu.VMEM((GROUP, D), BF16),
            pltpu.VMEM((GROUP, D), BF16),
        ],
        wait,
        in_specs=[SMEM] + [WHOLE] * 6,
        out_specs=(WHOLE,) * 5,
    )


def middle_kernel(at_ref, p0, p1, p3, token_ref, gain_ref, mid_ref, normed_ref):
    branch = p0[...].astype(F32) + p1[...].astype(F32) + p3[...].astype(F32)
    mid = token_ref[...].astype(F32) + branch
    mid_ref[...] = mid
    normed_ref[...] = (mid * inverse_rms(mid) * gain_ref[...]).astype(BF16)


def middle(order, at, parts, tokens, gain, wait):
    return order.call(
        middle_kernel,
        "middle",
        (like(TOK, D, dtype=F32), like(TOK, D)),
        (at, *parts, tokens, gain[None, :]),
        wait=wait,
        in_specs=[SMEM] + [WHOLE] * 5,
        out_specs=(WHOLE, WHOLE),
    )


RING = ((0, TOK), (TOK, TOK), (2 * TOK, TOK // 2), (2 * TOK + TOK // 2, TOK // 2), (3 * TOK, TOK))
RING_SPECS = [spec(count, D) for _, count in RING]


def feed_kernel(at_ref, *refs):
    blocks, cot_refs, weight_refs = refs[:5], refs[5:10], refs[10:12]
    (hidden_ref, gate_ref, up_ref), outs = refs[12:15], refs[15:20]
    rows, cots, weights, downs, total, gate_up_sems, down_sems = refs[20:]

    def gate_up_copy(z, own):
        return pltpu.make_async_copy(
            weight_refs[own].at[z, pl.ds(0, 2 * HID)], weights.at[z, own], gate_up_sems.at[z, own]
        )

    def down_copy(z, own):
        return pltpu.make_async_copy(
            weight_refs[own].at[z, pl.ds(2 * HID, HID)],
            downs.at[z, :, pl.ds(own * 1024, 1024)],
            down_sems.at[z, own],
        )

    for z in range(4):
        for own in (0, 1):
            gate_up_copy(z, own).start()
            down_copy(z, own).start()
    for (first, count), block, cot_ref in zip(RING, blocks, cot_refs):
        at = slice(first, first + count)
        for own in (0, 1):
            rows[own, at, :] = block[:, half_at(at_ref, own == 0)]
            cots[at, own * 1024 : (own + 1) * 1024] = cot_ref[:, half_at(at_ref, own == 0)]
    for z in range(4):
        for own in (0, 1):
            gate_up_copy(z, own).wait()
            down_copy(z, own).wait()
        both_rows = nt(weights[z, 0], rows[0]) + nt(weights[z, 1], rows[1])
        gate_rows, up_rows = both_rows[:HID], both_rows[HID:]
        grad_hidden = nt(downs[z], cots[...])
        sigmoid_gate = 1.0 / (1.0 + jnp.exp(-gate_rows))
        silu_gate = gate_rows * sigmoid_gate
        hidden_ref[z] = (silu_gate * up_rows).astype(BF16)
        up_delta = (grad_hidden * silu_gate).astype(BF16)
        gate_delta = (
            grad_hidden * up_rows * (sigmoid_gate + silu_gate * (1.0 - sigmoid_gate))
        ).astype(BF16)
        gate_ref[z] = gate_delta
        up_ref[z] = up_delta
        both_delta = jnp.concatenate([gate_delta, up_delta], axis=0)
        for own in (0, 1):
            part = tn(both_delta, weights[z, own])
            if z == 0:
                total[own] = part
            elif z < 3:
                total[own] += part
            else:
                part = (part + total[own]).astype(BF16)
                for (first, count), out_ref in zip(RING, outs):
                    out_ref[:, half_at(at_ref, own == 0)] = part[first : first + count]


def feed(order, at, second_blocks, cot_blocks, weights):
    deltas = like(4, HID, GROUP)
    return order.call(
        feed_kernel,
        "feed",
        (deltas, deltas, deltas) + RING_LIKE,
        (at, *second_blocks, *cot_blocks, *weights),
        [
            pltpu.VMEM((2, GROUP, 1024), BF16),
            pltpu.VMEM((GROUP, D), BF16),
            pltpu.VMEM((4, 2, 2 * HID, 1024), BF16),
            pltpu.VMEM((4, HID, D), BF16),
            pltpu.VMEM((2, GROUP, 1024), F32),
            pltpu.SemaphoreType.DMA((4, 2)),
            pltpu.SemaphoreType.DMA((4, 2)),
        ],
        in_specs=[SMEM] + [WHOLE] * 10 + [pl.BlockSpec(memory_space=pl.ANY)] * 2,
        out_specs=(WHOLE,) * 8,
    )


def down_kernel(at_ref, hidden_ref, own_ref, other_ref, *refs):
    out_ref, rows, downs, sems = refs

    def copy(own):
        weight_ref = own_ref if own == 0 else other_ref
        return pltpu.make_async_copy(
            weight_ref.at[:, pl.ds(2 * HID, HID)], downs.at[own], sems.at[own]
        )

    copy(0).start()
    copy(1).start()
    for z in range(4):
        rows[z] = jnp.transpose(hidden_ref[z].astype(F32)).astype(BF16)
    for own in (0, 1):
        copy(own).wait()
        part = nn(rows[0], downs[own, 0])
        for z in range(1, 4):
            part = part + nn(rows[z], downs[own, z])
        part = part.astype(BF16)
        for b in range(4):
            block = part[b * TOK : (b + 1) * TOK]
            out_ref[(at_ref[3] + b) % 4, :, half_at(at_ref, own == 0)] = block


def down(order, at, hidden, weights, wait):
    return order.call(
        down_kernel,
        "down",
        like(4, TOK, D),
        (at, hidden, *weights),
        [
            pltpu.VMEM((4, GROUP, HID), BF16),
            pltpu.VMEM((2, 4, HID, 1024), BF16),
            pltpu.SemaphoreType.DMA((2,)),
        ],
        wait,
        in_specs=[SMEM, WHOLE] + [pl.BlockSpec(memory_space=pl.ANY)] * 2,
        out_specs=WHOLE,
    )


def feed_grads_kernel(own, count, at_ref, *refs):
    lefts, blocks, rows = refs[:count], refs[count : count + 5], refs[-1]
    others, out_ref = refs[count + 5 : -2], refs[-2]
    step = pl.program_id(0)

    @pl.when(step == 0)
    def _():
        core = at_ref[1] if own else 1 - at_ref[1]
        for (first, size), block in zip(RING, blocks):
            for k in range(4):
                columns = pl.ds(pl.multiple_of((k * 2 + core) * PIECE, PIECE), PIECE)
                rows[first : first + size, k * PIECE : (k + 1) * PIECE] = block[:, columns]

    for i, left_ref in enumerate(lefts):
        part = nn(left_ref[0], rows[...])
        at = slice(i * HID, (i + 1) * HID)
        for k in range(4):
            block = part[:, k * PIECE : (k + 1) * PIECE]
            if own:
                block = block + others[0][k, 0, at, :].astype(F32)
            out_ref[k, 0, at, :] = block.astype(BF16)


def feed_grads(order, at, lefts, blocks, ahead, other=(), wait=()):
    own, count = bool(other), len(lefts)
    rows = count * HID

    def place(i, at_ref):
        return (i + 4 - at_ref[2]) % 4 if ahead else i

    grads = pl.BlockSpec((4, 1, rows, PIECE), lambda i, at_ref: (0, place(i, at_ref), 0, 0))
    return order.call(
        lambda *refs: feed_grads_kernel(own, count, *refs),
        "feed_grads_own" if own else "feed_grads",
        (like(4, 4, rows, PIECE),),
        (at, *lefts, *blocks, *other),
        wait=wait,
        grid_spec=pltpu.PrefetchScalarGridSpec(
            num_scalar_prefetch=1,
            grid=(4,),
            in_specs=[pl.BlockSpec((1, HID, GROUP), lambda i, at_ref: (i, 0, 0))] * count
            + [pl.BlockSpec((size, D), lambda i, at_ref: (0, 0)) for _, size in RING]
            + ([grads] if own else []),
            out_specs=(grads,),
            scratch_shapes=[pltpu.VMEM((GROUP, 1024), BF16)],
        ),
    )


def turn_kernel(
    at_ref, s0, s1, s3, mid_ref, cot_ref, gain_ref, branch_ref, grad_mid_ref, gain_part_ref
):
    grad_second = s0[...].astype(F32) + s1[...].astype(F32) + s3[...].astype(F32)
    mid = mid_ref[...]
    inverse = inverse_rms(mid)
    unit = mid * inverse
    gain_part_ref[...] = jnp.sum(grad_second * unit, axis=0, keepdims=True)
    grad_mid = cot_ref[...].astype(F32) + norm_back(grad_second, unit, inverse, gain_ref[...])
    grad_mid_ref[...] = grad_mid
    branch_ref[...] = grad_mid.astype(BF16)


def turn(order, at, second_sums, mid_rows, out_grad, gain):
    return order.call(
        turn_kernel,
        "turn",
        (like(TOK, D), like(TOK, D, dtype=F32), like(1, D, dtype=F32)),
        (at, *second_sums, mid_rows, out_grad, gain[None, :]),
        in_specs=[SMEM] + [WHOLE] * 6,
        out_specs=(WHOLE,) * 3,
    )


def back_kernel(at_ref, b0, b1, b2a, b2b, b3, own_ref, other_ref, *refs):
    outs, rows_ref, weights = refs[:4], refs[4], refs[5]
    for block_ref, (d, first, count) in zip((b0, b1, b2a, b2b, b3), RING_ROWS):
        at = pl.ds(pl.multiple_of((at_ref[3] + d) % 4 * TOK + first, count), count)
        rows_ref[at, :] = block_ref[...]
    for d in range(4):
        head_weights(at_ref, own_ref, other_ref, weights, d)
    total = nt(weights[...], rows_ref[...]).astype(BF16)
    for d, out_ref in enumerate(outs):
        out_ref[...] = total[d * HEAD_V : (d + 1) * HEAD_V, :]


def back_projection(order, at, branch_blocks, weights):
    return order.call(
        back_kernel,
        "back_projection",
        (like(HEAD_V, GROUP),) * 4 + (like(GROUP, D),),
        (at, *branch_blocks, *weights),
        [pltpu.VMEM((GROUP, D), BF16)],
        in_specs=[SMEM] + [WHOLE] * 7,
        out_specs=(WHOLE,) * 5,
    )


def own_first(at_ref, out, block, rows):
    for own in (0, 1):
        for k in range(4):
            columns = pl.ds(piece_at(at_ref, k, own == 0), PIECE)
            piece = own * 4 + k
            out[rows, piece * PIECE : (piece + 1) * PIECE] = block[:, columns]


def out_grads_kernel(at_ref, m0, m1, m2, m3, branch_ref, out_ref, rows):
    own_first(at_ref, rows, branch_ref, slice(0, GROUP))
    for back, mixed_ref in enumerate((m0, m1, m2, m3)):
        out_ref[(4 - back) % 4] = nn(mixed_ref[...], rows[...]).astype(BF16)


def out_grads(order, at, mixed, branch_rows):
    return order.call(
        out_grads_kernel,
        "out_grads",
        like(4, HEAD_V, D),
        (at, *mixed, branch_rows),
        [pltpu.VMEM((GROUP, D), BF16)],
        in_specs=[SMEM] + [WHOLE] * 5,
        out_specs=WHOLE,
    )


BOTH_ROWS = HEAD_V + HEAD_ROWS + 16


def head_grads_kernel(at_ref, *refs):
    (g0, g1, g2, g3), weights, normed_ref, gain_ref = refs[:4], refs[4:9], refs[9], refs[10]
    out_grad_ref, second_ref, own_ref, other_ref, rows = refs[11:]
    own_first(at_ref, rows, normed_ref, slice(0, GROUP))
    rest = HEAD_ROWS - HALF_ROWS
    places = (
        (g0, ((weights[0], HEAD_ROWS),)),
        (g3, ((weights[1], HEAD_ROWS),)),
        (g2, ((weights[2], HALF_ROWS), (weights[3], rest))),
        (g1, ((weights[4], HEAD_ROWS),)),
    )
    for own in (0, 1):
        sent_ref = own_ref if own == 0 else other_ref
        for k in range(4):
            columns = pl.ds(piece_at(at_ref, k, own == 0), PIECE)
            piece = slice((own * 4 + k) * PIECE, (own * 4 + k + 1) * PIECE)
            gain_part = jnp.zeros((1, PIECE), F32)
            for d, (grads_ref, w_refs) in enumerate(places):
                part = nn(grads_ref[...], rows[:, piece])
                first = 0
                for w_ref, count in w_refs:
                    weighted = part[first : first + count] * w_ref[:count, columns].astype(F32)
                    gain_part = gain_part + jnp.sum(weighted, axis=0, keepdims=True)
                    first += count
                sent_ref[d, k, :HEAD_V] = out_grad_ref[d, :, piece]
                sent_ref[d, k, HEAD_V : HEAD_V + HEAD_ROWS] = part.astype(BF16)
            gain_part = gain_part / gain_ref[:, columns]
            gain_rows = jnp.where(
                lax.broadcasted_iota(jnp.int32, (16, PIECE), 0) == 0,
                gain_part,
                second_ref[:, columns],
            ).astype(BF16)
            for d in range(4):
                sent_ref[d, k, HEAD_V + HEAD_ROWS :] = gain_rows


def head_grads(order, at, grads, head_blocks, normed, gain, out_part, second_part, wait):
    both = like(4, 4, BOTH_ROWS, PIECE)
    return order.call(
        head_grads_kernel,
        "head_grads",
        (both, both),
        (at, *grads, *head_blocks, normed, gain[None, :], out_part, second_part),
        [pltpu.VMEM((GROUP, D), BF16)],
        wait,
        in_specs=[SMEM] + [WHOLE] * 13,
        out_specs=(WHOLE,) * 2,
    )


def add_kernel(at_ref, mine_ref, other_ref, *outs):
    for d, out_ref in enumerate(outs):
        out_ref[...] = (mine_ref[d].astype(F32) + other_ref[d].astype(F32)).astype(BF16)


def add_blocks(order, at, mine, other):
    return order.call(
        add_kernel,
        "add_blocks",
        (like(4, BOTH_ROWS, PIECE),) * 4,
        (at, mine, other),
        in_specs=[SMEM] + [WHOLE] * 2,
        out_specs=(WHOLE,) * 4,
    )


def first_kernel(at_ref, *refs):
    grads, (w0, w1, w2a, w2b, w3), outs = refs[:4], refs[4:9], refs[9:14]
    rest = HEAD_ROWS - HALF_ROWS
    for d in range(4):
        columns = at_place(at_ref, d)
        part = tn(grads[0][:, columns], w0[:HEAD_ROWS, :])
        part = part + tn(grads[3][:, columns], w1[:HEAD_ROWS, :])
        part = part + tn(grads[1][:, columns], w3[:HEAD_ROWS, :])
        part = part + tn(grads[2][:HALF_ROWS, columns], w2a[...])
        part = (part + tn(grads[2][HALF_ROWS:, columns], w2b[:rest, :])).astype(BF16)
        for out_ref, (place, first, count) in zip(outs, RING_ROWS):
            if place == d:
                out_ref[...] = part[first : first + count]


def first_part(order, at, grads, head_blocks, wait):
    return order.call(
        first_kernel,
        "first_part",
        RING_LIKE,
        (at, *grads, *head_blocks),
        wait=wait,
        in_specs=[SMEM] + [WHOLE] * 9,
        out_specs=(WHOLE,) * 5,
    )


def collect_kernel(turned, at_ref, *refs):
    outs = refs[5:]
    for own in (True, False):
        for d in range(4):
            columns = pl.ds(piece_at(at_ref, d, own), PIECE)
            first = 0
            for i, out_ref in enumerate(outs):
                rows = out_ref.shape[1 if i == turned else 0]
                at = slice(first, first - (-rows // 16 * 16))
                block = (refs[d][at, :] if own else refs[4][d, at, :]).astype(F32)[:rows]
                if i == turned:
                    out_ref[columns, :] = jnp.transpose(block)
                else:
                    out_ref[:, columns] = block
                first += -rows // 16 * -16


def collect(order, at, mine, name, *rows, turned=None):
    other = swapped(jnp.stack(mine))
    return order.call(
        lambda *refs: collect_kernel(turned, *refs),
        name,
        tuple(
            like(D, r, dtype=F32) if i == turned else like(r, D, dtype=F32)
            for i, r in enumerate(rows)
        ),
        (at, *mine, other),
        in_specs=[SMEM] + [WHOLE] * 5,
        out_specs=(WHOLE,) * len(rows),
    )


def after(array, *needed):
    return lax.optimization_barrier((array, *needed))[0]


def body(
    tokens,
    doc_start,
    gain_first,
    w_query,
    w_key,
    w_value,
    w_out,
    gain_second,
    w_gate,
    w_up,
    w_down,
    out_grad,
):
    order = Order()
    at = jnp.stack([lax.axis_index(a) for a in AXES]).astype(jnp.int32)
    x_at, core, z_at, y_at = (at[i] for i in range(4))

    token_blocks = ring_gathered(tokens, "y")
    out_half = lax.dynamic_slice_in_dim(w_out, core * (HEAD_V // 2), HEAD_V // 2, 0)
    w_head = jnp.concatenate([w_query.T, w_key.T, w_value.T, out_half], axis=0)
    head_blocks = ring_gathered(w_head, "z")
    feed_half = jnp.concatenate([w_gate.T, w_up.T, w_down], axis=0)
    feed_half = lax.dynamic_slice_in_dim(feed_half, core * 1024, 1024, 1)
    *qkv, group_normed = project(order, at, token_blocks, head_blocks, gain_first, ())
    feed_half = after(feed_half, *token_blocks[2:4], *head_blocks[2:4])
    feed_mine = lax.all_gather(feed_half, "z", axis=0)
    qkv = exchanged(qkv, "z")
    out_mine = jnp.stack([block[-(HEAD_V // 2) :] for block in (*head_blocks[:2], *head_blocks[3:])])
    out_mine = after(out_mine, *qkv)
    out_weights = (out_mine, swapped(out_mine))
    cot_rows = jnp.broadcast_to(after(out_grad, group_normed)[None], (4, TOK, D))
    cot_rows = lax.all_to_all(cot_rows, "y", 0, 0)

    positions = jnp.arange(SEQ, dtype=jnp.int32)
    start_row = lax.cummax(jnp.where(doc_start != 0, positions, 0))[None, :]
    *mixed, numer, denom, qkv = attention_forward(order, at, qkv, start_row, ())
    mixed = exchanged(mixed, "z")
    p0, p1, *p2, p3 = out_projection(order, at, mixed, out_weights, (cot_rows,))
    parts = (p0, *ring_end(ring_start(p2, "y"), p1, p3, "y"))
    mid_rows, second_normed = middle(order, at, parts, tokens, gain_second, ())

    cot_blocks = [out_grad] + [
        lax.dynamic_slice(cot_rows, ((y_at + d) % 4, first, 0), (1, count, D))[0]
        for d, first, count in RING_ROWS[1:]
    ]
    second_blocks = ring_gathered(second_normed, "y")
    feed_mine = after(feed_mine, second_blocks[1], second_blocks[4])
    feed_weights = (feed_mine, swapped(feed_mine))
    hidden, gate_delta, up_delta, s0, s1, *s2, s3 = feed(
        order, at, second_blocks, cot_blocks, feed_weights
    )
    arrived = ring_start(s2, "y")
    second_sums = (s0, *ring_end(arrived, s1, s3, "y"))
    deltas = (gate_delta, up_delta)
    (gu_grads,) = feed_grads(order, at, deltas, second_blocks, False, wait=arrived)
    gu_grads = swapped(gu_grads)
    (down_grads,) = feed_grads(order, at, (hidden,), cot_blocks, True)
    down_grads = swapped(down_grads)

    grad_branch, grad_mid, gain_second_part = turn(
        order, at, second_sums, mid_rows, out_grad, gain_second
    )
    branch_blocks = ring_gathered(grad_branch, "y")
    (gu_grads,) = feed_grads(
        order,
        at,
        deltas,
        second_blocks,
        False,
        (gu_grads,),
        wait=(branch_blocks[1], branch_blocks[4]),
    )
    gu_sum = lax.psum_scatter(
        gu_grads.reshape(16, 2 * HID, PIECE), ("x", "z"), scatter_dimension=0
    )
    b_parts = down(order, at, hidden, feed_weights, ())
    *grad_mixed, branch_rows = back_projection(order, at, branch_blocks, out_weights)
    grad_mixed = exchanged(grad_mixed, "z")
    b_parts = lax.all_to_all(after(b_parts, branch_rows), "y", 0, 0)
    (down_grads,) = feed_grads(order, at, (hidden,), cot_blocks, True, (down_grads,))
    out_part = out_grads(order, at, mixed, branch_rows)
    grads = attention_backward(order, at, qkv, grad_mixed, numer, denom, start_row, ())
    grads = exchanged(grads, "z")

    def added(blocks):
        total = (blocks[0].astype(F32) + blocks[1].astype(F32)) + (
            blocks[2].astype(F32) + blocks[3].astype(F32)
        )
        return total.astype(BF16)

    mine, other = head_grads(
        order,
        at,
        grads,
        head_blocks,
        group_normed,
        gain_first,
        out_part,
        gain_second_part,
        (b_parts,),
    )
    down_grads = lax.all_to_all(after(down_grads, b_parts), "x", 0, 0)
    other = swapped(other)
    f0, f1, *f2, f3 = first_part(order, at, grads, head_blocks, ())
    head_part = added(exchanged(add_blocks(order, at, mine, other), "z"))
    f_arrived = ring_start(f2, "y")
    head_part = after(head_part, *f_arrived)
    from_back, from_ahead = ring_end(f_arrived, f1, f3, "y")
    gu_blocks = gathered(gu_sum, "x")
    head_part = after(head_part, *gu_blocks[1:])
    head_sum = added(exchanged([head_part[d] for d in range(4)], "x"))
    down_grads = after(down_grads, *gu_blocks[1:])
    down_part = jnp.sum(down_grads.astype(F32), axis=0).astype(BF16)
    down_sum = added(exchanged([down_part[d] for d in range(4)], "z"))
    grad_first = f0.astype(F32) + from_back.astype(F32) + from_ahead.astype(F32)
    block_out = mid_rows + jnp.sum(b_parts.astype(F32), axis=0)
    x_rows = tokens.astype(F32)
    first_inv = inverse_rms(x_rows)
    input_grad = grad_mid + norm_back(grad_first, x_rows * first_inv, first_inv, gain_first)

    grad_gate, grad_up = collect(order, at, gu_blocks, "collect_gate_up", HID, HID)
    rest_sum = jnp.concatenate([head_sum, down_sum], axis=0)
    rest_sum = after(rest_sum, grad_gate, from_back, from_ahead)
    grad_out, grad_query, grad_key, grad_value, gains, grad_down = collect(
        order,
        at,
        gathered(rest_sum, "x"),
        "collect_rest",
        HEAD_V,
        FEAT,
        FEAT,
        HEAD_V,
        2,
        HID,
        turned=3,
    )
    gains = gathered(gains, "y")
    gains = (gains[0] + gains[1]) + (gains[2] + gains[3])
    return (
        block_out,
        input_grad,
        gains[0],
        grad_query.T,
        grad_key.T,
        grad_value,
        grad_out,
        gains[1],
        grad_gate.T,
        grad_up.T,
        grad_down,
    )


def solution(mesh):
    fine = Mesh(mesh.devices.reshape(4, 2, 4, 4), AXES)
    rows, dp, mp = P(AXES, None), P(("x", "core")), ("z", "y")
    return jax.shard_map(
        body,
        mesh=fine,
        in_specs=(
            rows,
            dp,
            P(),
            P(None, mp),
            P(None, mp),
            P(None, mp),
            P(mp, None),
            P(),
            P(None, mp),
            P(None, mp),
            P(mp, None),
            rows,
        ),
        out_specs=(
            rows,
            rows,
            P(),
            P(None, mp),
            P(None, mp),
            P(None, mp),
            P(mp, None),
            P(),
            P(None, mp),
            P(None, mp),
            P(mp, None),
        ),
        check_vma=False,
    )
```

```python
import jax
import jax.numpy as jnp
from jax import lax
from jax.experimental import pallas as pl
from jax.experimental.pallas import tpu as pltpu
from jax.sharding import Mesh, PartitionSpec as P

FEAT = 16
HEAD_V = 128
EPS = 1e-05
F32 = jnp.float32
BF16 = jnp.bfloat16
TOK = 128
GROUP = 512
SEQ = 2048
HEAD_ROWS = 2 * FEAT + HEAD_V
AXES = ("x", "core", "z", "y")
D = 2048
HID = 352
PIECE = 256


def shifted(array, axis, by):
    return lax.ppermute(array, axis, [(i, (i + by) % 4) for i in range(4)])


def swapped(array):
    return lax.ppermute(array, "core", [(0, 1), (1, 0)])


def swapped_each(arrays):
    return [swapped(array) for array in arrays]


def gathered(array, axis):
    return [
        array,
        shifted(array, axis, 3),
        shifted(array, axis, 2),
        shifted(array, axis, 1),
    ]


def ring_gathered(array, axis):
    half = array.shape[0] // 2
    ahead, back = shifted(array, axis, 3), shifted(array, axis, 1)
    return [array, ahead, shifted(back[:half], axis, 1), shifted(ahead[half:], axis, 3), back]


def ring_start(opposite, axis):
    return shifted(opposite[0], axis, 1), shifted(opposite[1], axis, 3)


def ring_end(arrived, ahead, back, axis):
    half = ahead.shape[0] // 2
    first, second = arrived
    ahead = jnp.concatenate([ahead[:half] + first, ahead[half:]], axis=0)
    back = jnp.concatenate([back[:half], back[half:] + second], axis=0)
    return shifted(ahead, axis, 1), shifted(back, axis, 3)


def exchanged(blocks, axis):
    return [
        blocks[0],
        shifted(blocks[1], axis, 1),
        shifted(blocks[2], axis, 2),
        shifted(blocks[3], axis, 3),
    ]


def in_order(blocks, at):
    stacked = jnp.stack(blocks)
    return jnp.concatenate(
        [lax.dynamic_index_in_dim(stacked, (j - at) % 4, 0, keepdims=False) for j in range(4)], axis=0
    )


def nn(left, right):
    return jnp.dot(left, right, preferred_element_type=F32)


def nt(left, right):
    return lax.dot_general(left, right, (((1,), (1,)), ((), ())), preferred_element_type=F32)


def tn(left, right):
    return lax.dot_general(left, right, (((0,), (0,)), ((), ())), preferred_element_type=F32)


def pair_mask(start_row, si, ti, first, rows):
    row = lax.broadcasted_iota(jnp.int32, (rows, GROUP), 0) + (si * GROUP + first)
    mask = row >= start_row
    if si == ti:
        column = lax.broadcasted_iota(jnp.int32, (rows, GROUP), 1) + ti * GROUP
        mask = mask & (row <= column)
    return mask


def forward_kernel(
    at_ref,
    q0,
    q1,
    q2,
    q3,
    start_ref,
    m0,
    m1,
    m2,
    m3,
    numer_ref,
    denom_ref,
    qkv_ref,
    mixed_ref,
    keys,
):
    for d, ref in enumerate((q0, q1, q2, q3)):
        qkv_ref[(at_ref[2] + 4 - d) % 4] = ref[...]
    for si in range(4):
        keys[si] = jnp.transpose(qkv_ref[si, FEAT : 2 * FEAT, :].astype(F32)).astype(BF16)
    for ti in range(4):
        query = (qkv_ref[ti, 0:FEAT, :].astype(F32) * (FEAT**-0.5)).astype(BF16)
        start_row = start_ref[:, ti * GROUP : (ti + 1) * GROUP]
        numer = jnp.zeros((HEAD_V, GROUP), F32)
        denom = jnp.zeros((1, GROUP), F32)
        for si in range(ti + 1):
            one = nn(keys[si], query) + 1.0
            weight = jnp.where(
                pair_mask(start_row, si, ti, 0, GROUP), 0.5 * (one * one) + 0.5, 0.0
            )
            denom = denom + jnp.sum(weight, axis=0, keepdims=True)
            numer = numer + nn(qkv_ref[si, 2 * FEAT :, :], weight.astype(BF16))
        numer_ref[ti] = numer
        denom_ref[ti] = denom
        mixed_ref[ti] = (numer / denom).astype(BF16)
    for d, ref in enumerate((m0, m1, m2, m3)):
        ref[...] = mixed_ref[(at_ref[2] + d) % 4]


def attention_forward(order, at, qkv, start_row, wait):
    return order.call(
        forward_kernel,
        "attention_forward",
        (like(HEAD_V, GROUP),) * 4
        + (
            like(4, HEAD_V, GROUP, dtype=F32),
            like(4, 1, GROUP, dtype=F32),
            like(4, HEAD_ROWS, GROUP),
        ),
        (at, *qkv, start_row),
        [pltpu.VMEM((4, HEAD_V, GROUP), BF16), pltpu.VMEM((4, GROUP, FEAT), BF16)],
        wait,
        in_specs=[SMEM] + [WHOLE] * 5,
        out_specs=(WHOLE,) * 7,
    )


def backward_kernel(
    at_ref,
    c0,
    c1,
    c2,
    c3,
    qkv_ref,
    numer_ref,
    denom_ref,
    start_ref,
    g0,
    g1,
    g2,
    g3,
    out_ref,
    cot_ref,
    keys,
    values,
    key_sum,
    value_sum,
):
    for d, ref in enumerate((c0, c1, c2, c3)):
        cot_ref[(at_ref[2] + 4 - d) % 4] = ref[...]
    for si in range(4):
        keys[si] = jnp.transpose(qkv_ref[si, FEAT : 2 * FEAT, :].astype(F32)).astype(BF16)
        values[si] = jnp.transpose(qkv_ref[si, 2 * FEAT :, :].astype(F32)).astype(BF16)
    key_sum[...] = jnp.zeros_like(key_sum)
    value_sum[...] = jnp.zeros_like(value_sum)
    for ti in range(4):
        query_f32 = qkv_ref[ti, 0:FEAT, :].astype(F32) * (FEAT**-0.5)
        query = query_f32.astype(BF16)
        query_rows = jnp.transpose(query_f32).astype(BF16)
        start_row = start_ref[:, ti * GROUP : (ti + 1) * GROUP]
        inverse = 1.0 / denom_ref[ti]
        cot = cot_ref[ti].astype(F32)
        cot_denom = -jnp.sum(cot * numer_ref[ti], axis=0, keepdims=True) * (inverse * inverse)
        cot_f32 = cot * inverse
        cot_numer = cot_f32.astype(BF16)
        cot_rows = jnp.transpose(cot_f32).astype(BF16)
        query_sum = jnp.zeros((FEAT, GROUP), F32)
        for si in range(ti + 1):
            one = nn(keys[si], query) + 1.0
            mask = pair_mask(start_row, si, ti, 0, GROUP)
            weight = jnp.where(mask, 0.5 * (one * one) + 0.5, 0.0).astype(BF16)
            value_sum[si] += nn(weight, cot_rows)
            cot_weight = nn(values[si], cot_numer) + cot_denom
            cot_score = jnp.where(mask, cot_weight * one, 0.0).astype(BF16)
            key_sum[si] += nn(cot_score, query_rows)
            query_sum = query_sum + nn(qkv_ref[si, FEAT : 2 * FEAT, :], cot_score)
        out_ref[ti, 0:FEAT, :] = (query_sum * (FEAT**-0.5)).astype(BF16)
    for si in range(4):
        out_ref[si, FEAT : 2 * FEAT, :] = jnp.transpose(key_sum[si]).astype(BF16)
        out_ref[si, 2 * FEAT :, :] = jnp.transpose(value_sum[si]).astype(BF16)
    for d, ref in enumerate((g0, g1, g2, g3)):
        ref[...] = out_ref[(at_ref[2] + d) % 4]


def attention_backward(order, at, qkv, cot, numer, denom, start_row, wait):
    return order.call(
        backward_kernel,
        "attention_backward",
        (like(HEAD_ROWS, GROUP),) * 4,
        (at, *cot, qkv, numer, denom, start_row),
        [
            pltpu.VMEM((4, HEAD_ROWS, GROUP), BF16),
            pltpu.VMEM((4, HEAD_V, GROUP), BF16),
            pltpu.VMEM((4, GROUP, FEAT), BF16),
            pltpu.VMEM((4, GROUP, HEAD_V), BF16),
            pltpu.VMEM((4, GROUP, FEAT), F32),
            pltpu.VMEM((4, GROUP, HEAD_V), F32),
        ],
        wait,
        in_specs=[SMEM] + [WHOLE] * 8,
        out_specs=(WHOLE,) * 4,
    )


VMEM_LIMIT = 52 * 2**20


class Order:
    def __init__(self):
        self.last = ()

    def call(self, kernel, name, out_shape, args, scratch=(), wait=(), **specs):
        at, first, *rest = args
        first = lax.optimization_barrier((first, *self.last, *wait))[0]
        if "grid_spec" not in specs:
            specs["scratch_shapes"] = list(scratch)
        out = pl.pallas_call(
            kernel,
            out_shape=out_shape,
            compiler_params=pltpu.CompilerParams(vmem_limit_bytes=VMEM_LIMIT),
            cost_estimate=pl.CostEstimate(flops=1, bytes_accessed=1, transcendentals=0),
            name=name,
            **specs,
        )(at, first, *rest)
        self.last = (out[0] if isinstance(out, (tuple, list)) else out,)
        return out


SMEM = pl.BlockSpec(memory_space=pltpu.SMEM)
WHOLE = pl.BlockSpec(memory_space=pltpu.VMEM)


def spec(*shape, at=None):
    def index(i):
        return tuple(i if k == at else 0 for k in range(len(shape)))

    return pl.BlockSpec(shape, index)


def like(*shape, dtype=BF16):
    return jax.ShapeDtypeStruct(shape, dtype)


def piece_at(at_ref, place, own_core):
    core = at_ref[1] if own_core else 1 - at_ref[1]
    return pl.multiple_of(((at_ref[0] + place) % 4 * 2 + core) * PIECE, PIECE)


def inverse_rms(rows):
    return lax.rsqrt(jnp.mean(rows * rows, axis=1, keepdims=True) + EPS)


def norm_back(grad_normed, unit, inverse, gains):
    scaled = grad_normed * gains
    return inverse * (scaled - unit * jnp.mean(scaled * unit, axis=1, keepdims=True))


RING_ROWS = ((0, 0, TOK), (1, 0, TOK), (2, 0, TOK // 2), (2, TOK // 2, TOK // 2), (3, 0, TOK))


HALF_ROWS = (HEAD_ROWS + HEAD_V // 2) // 2


def project_kernel(at_ref, *refs):
    tokens, weights, gain_ref = refs[:5], refs[5:10], refs[10]
    outs, normed_ref = refs[11:15], refs[15]
    for token_ref, (d, first, count) in zip(tokens, RING_ROWS):
        rows = token_ref[...].astype(F32)
        normed = (rows * inverse_rms(rows) * gain_ref[...]).astype(BF16)
        at = pl.multiple_of((at_ref[3] + d) % 4 * TOK, TOK) + first
        normed_ref[pl.ds(pl.multiple_of(at, count), count), :] = normed
    normed = normed_ref[...]
    for d, w_ref in ((0, weights[0]), (1, weights[1]), (3, weights[4])):
        outs[d][...] = nt(w_ref[:HEAD_ROWS, :], normed).astype(BF16)
    outs[2][:HALF_ROWS, :] = nt(weights[2][...], normed).astype(BF16)
    outs[2][HALF_ROWS:, :] = nt(weights[3][: HEAD_ROWS - HALF_ROWS, :], normed).astype(BF16)


def project(order, at, token_blocks, head_blocks, gain, wait):
    return order.call(
        project_kernel,
        "project",
        (like(HEAD_ROWS, GROUP),) * 4 + (like(GROUP, D),),
        (at, *token_blocks, *head_blocks, gain[None, :]),
        wait=wait,
        in_specs=[SMEM] + [WHOLE] * 11,
        out_specs=(WHOLE,) * 5,
    )


def half_at(at_ref, own):
    core = at_ref[1] if own else 1 - at_ref[1]
    return pl.ds(pl.multiple_of(core * 1024, 1024), 1024)


RING_LIKE = tuple(like(count, D) for _, _, count in RING_ROWS)


def at_place(at_ref, d):
    return pl.ds(pl.multiple_of((at_ref[3] + d) % 4 * TOK, TOK), TOK)


def out_kernel(at_ref, m0, m1, m2, m3, own_ref, other_ref, *refs):
    outs, (mixed, rows, weights) = refs[:5], refs[5:]
    for d, mixed_ref in enumerate((m0, m3, m2, m1)):
        mixed[:, d * HEAD_V : (d + 1) * HEAD_V] = jnp.transpose(mixed_ref[...].astype(F32)).astype(
            BF16
        )
        head_weights(at_ref, own_ref, other_ref, weights, d)
    rows[...] = nn(mixed[...], weights[...]).astype(BF16)
    for out_ref, (d, first, count) in zip(outs, RING_ROWS):
        at = pl.multiple_of((at_ref[3] + d) % 4 * TOK + first, count)
        out_ref[...] = rows[pl.ds(at, count), :]


def head_weights(at_ref, own_ref, other_ref, weights, d):
    half = HEAD_V // 2
    for core, w_ref in ((at_ref[1], own_ref), (1 - at_ref[1], other_ref)):
        first = pl.multiple_of(d * HEAD_V + core * half, half)
        weights[pl.ds(first, half), :] = w_ref[d]


def out_projection(order, at, mixed, weights, wait):
    return order.call(
        out_kernel,
        "out_projection",
        RING_LIKE,
        (at, *mixed, *weights),
        [
            pltpu.VMEM((GROUP, GROUP), BF16),
            pltpu.VMEM((GROUP, D), BF16),
            pltpu.VMEM((GROUP, D), BF16),
        ],
        wait,
        in_specs=[SMEM] + [WHOLE] * 6,
        out_specs=(WHOLE,) * 5,
    )


def middle_kernel(at_ref, p0, p1, p3, token_ref, gain_ref, mid_ref, normed_ref):
    branch = p0[...].astype(F32) + p1[...].astype(F32) + p3[...].astype(F32)
    mid = token_ref[...].astype(F32) + branch
    mid_ref[...] = mid
    normed_ref[...] = (mid * inverse_rms(mid) * gain_ref[...]).astype(BF16)


def middle(order, at, parts, tokens, gain, wait):
    return order.call(
        middle_kernel,
        "middle",
        (like(TOK, D, dtype=F32), like(TOK, D)),
        (at, *parts, tokens, gain[None, :]),
        wait=wait,
        in_specs=[SMEM] + [WHOLE] * 5,
        out_specs=(WHOLE, WHOLE),
    )


RING = ((0, TOK), (TOK, TOK), (2 * TOK, TOK // 2), (2 * TOK + TOK // 2, TOK // 2), (3 * TOK, TOK))
RING_SPECS = [spec(count, D) for _, count in RING]


def feed_kernel(at_ref, *refs):
    blocks, cot_refs, weight_refs = refs[:5], refs[5:10], refs[10:12]
    (hidden_ref, gate_ref, up_ref), outs = refs[12:15], refs[15:20]
    rows, cots, weights, downs, total, gate_up_sems, down_sems = refs[20:]

    def gate_up_copy(z, own):
        return pltpu.make_async_copy(
            weight_refs[own].at[z, pl.ds(0, 2 * HID)], weights.at[z, own], gate_up_sems.at[z, own]
        )

    def down_copy(z, own):
        return pltpu.make_async_copy(
            weight_refs[own].at[z, pl.ds(2 * HID, HID)],
            downs.at[z, :, pl.ds(own * 1024, 1024)],
            down_sems.at[z, own],
        )

    for z in range(4):
        for own in (0, 1):
            gate_up_copy(z, own).start()
            down_copy(z, own).start()
    for (first, count), block, cot_ref in zip(RING, blocks, cot_refs):
        at = slice(first, first + count)
        for own in (0, 1):
            rows[own, at, :] = block[:, half_at(at_ref, own == 0)]
            cots[at, own * 1024 : (own + 1) * 1024] = cot_ref[:, half_at(at_ref, own == 0)]
    for z in range(4):
        for own in (0, 1):
            gate_up_copy(z, own).wait()
            down_copy(z, own).wait()
        both_rows = nt(weights[z, 0], rows[0]) + nt(weights[z, 1], rows[1])
        gate_rows, up_rows = both_rows[:HID], both_rows[HID:]
        grad_hidden = nt(downs[z], cots[...])
        sigmoid_gate = 1.0 / (1.0 + jnp.exp(-gate_rows))
        silu_gate = gate_rows * sigmoid_gate
        hidden_ref[z] = (silu_gate * up_rows).astype(BF16)
        up_delta = (grad_hidden * silu_gate).astype(BF16)
        gate_delta = (
            grad_hidden * up_rows * (sigmoid_gate + silu_gate * (1.0 - sigmoid_gate))
        ).astype(BF16)
        gate_ref[z] = gate_delta
        up_ref[z] = up_delta
        both_delta = jnp.concatenate([gate_delta, up_delta], axis=0)
        for own in (0, 1):
            part = tn(both_delta, weights[z, own])
            if z == 0:
                total[own] = part
            elif z < 3:
                total[own] += part
            else:
                part = (part + total[own]).astype(BF16)
                for (first, count), out_ref in zip(RING, outs):
                    out_ref[:, half_at(at_ref, own == 0)] = part[first : first + count]


def feed(order, at, second_blocks, cot_blocks, weights):
    deltas = like(4, HID, GROUP)
    return order.call(
        feed_kernel,
        "feed",
        (deltas, deltas, deltas) + RING_LIKE,
        (at, *second_blocks, *cot_blocks, *weights),
        [
            pltpu.VMEM((2, GROUP, 1024), BF16),
            pltpu.VMEM((GROUP, D), BF16),
            pltpu.VMEM((4, 2, 2 * HID, 1024), BF16),
            pltpu.VMEM((4, HID, D), BF16),
            pltpu.VMEM((2, GROUP, 1024), F32),
            pltpu.SemaphoreType.DMA((4, 2)),
            pltpu.SemaphoreType.DMA((4, 2)),
        ],
        in_specs=[SMEM] + [WHOLE] * 10 + [pl.BlockSpec(memory_space=pl.ANY)] * 2,
        out_specs=(WHOLE,) * 8,
    )


def down_kernel(at_ref, hidden_ref, own_ref, other_ref, *refs):
    out_ref, rows, downs, sems = refs

    def copy(own):
        weight_ref = own_ref if own == 0 else other_ref
        return pltpu.make_async_copy(
            weight_ref.at[:, pl.ds(2 * HID, HID)], downs.at[own], sems.at[own]
        )

    copy(0).start()
    copy(1).start()
    for z in range(4):
        rows[z] = jnp.transpose(hidden_ref[z].astype(F32)).astype(BF16)
    for own in (0, 1):
        copy(own).wait()
        part = nn(rows[0], downs[own, 0])
        for z in range(1, 4):
            part = part + nn(rows[z], downs[own, z])
        part = part.astype(BF16)
        for b in range(4):
            block = part[b * TOK : (b + 1) * TOK]
            out_ref[(at_ref[3] + b) % 4, :, half_at(at_ref, own == 0)] = block


def down(order, at, hidden, weights, wait):
    return order.call(
        down_kernel,
        "down",
        like(4, TOK, D),
        (at, hidden, *weights),
        [
            pltpu.VMEM((4, GROUP, HID), BF16),
            pltpu.VMEM((2, 4, HID, 1024), BF16),
            pltpu.SemaphoreType.DMA((2,)),
        ],
        wait,
        in_specs=[SMEM, WHOLE] + [pl.BlockSpec(memory_space=pl.ANY)] * 2,
        out_specs=WHOLE,
    )


def feed_grads_kernel(own, count, at_ref, *refs):
    lefts, blocks, rows = refs[:count], refs[count : count + 5], refs[-1]
    others, out_ref = refs[count + 5 : -2], refs[-2]
    step = pl.program_id(0)

    @pl.when(step == 0)
    def _():
        core = at_ref[1] if own else 1 - at_ref[1]
        for (first, size), block in zip(RING, blocks):
            for k in range(4):
                columns = pl.ds(pl.multiple_of((k * 2 + core) * PIECE, PIECE), PIECE)
                rows[first : first + size, k * PIECE : (k + 1) * PIECE] = block[:, columns]

    for i, left_ref in enumerate(lefts):
        part = nn(left_ref[0], rows[...])
        at = slice(i * HID, (i + 1) * HID)
        for k in range(4):
            block = part[:, k * PIECE : (k + 1) * PIECE]
            if own:
                block = block + others[0][k, 0, at, :].astype(F32)
            out_ref[k, 0, at, :] = block.astype(BF16)


def feed_grads(order, at, lefts, blocks, ahead, other=(), wait=()):
    own, count = bool(other), len(lefts)
    rows = count * HID

    def place(i, at_ref):
        return (i + 4 - at_ref[2]) % 4 if ahead else i

    grads = pl.BlockSpec((4, 1, rows, PIECE), lambda i, at_ref: (0, place(i, at_ref), 0, 0))
    return order.call(
        lambda *refs: feed_grads_kernel(own, count, *refs),
        "feed_grads_own" if own else "feed_grads",
        (like(4, 4, rows, PIECE),),
        (at, *lefts, *blocks, *other),
        wait=wait,
        grid_spec=pltpu.PrefetchScalarGridSpec(
            num_scalar_prefetch=1,
            grid=(4,),
            in_specs=[pl.BlockSpec((1, HID, GROUP), lambda i, at_ref: (i, 0, 0))] * count
            + [pl.BlockSpec((size, D), lambda i, at_ref: (0, 0)) for _, size in RING]
            + ([grads] if own else []),
            out_specs=(grads,),
            scratch_shapes=[pltpu.VMEM((GROUP, 1024), BF16)],
        ),
    )


def turn_kernel(
    at_ref, s0, s1, s3, mid_ref, cot_ref, gain_ref, branch_ref, grad_mid_ref, gain_part_ref
):
    grad_second = s0[...].astype(F32) + s1[...].astype(F32) + s3[...].astype(F32)
    mid = mid_ref[...]
    inverse = inverse_rms(mid)
    unit = mid * inverse
    gain_part_ref[...] = jnp.sum(grad_second * unit, axis=0, keepdims=True)
    grad_mid = cot_ref[...].astype(F32) + norm_back(grad_second, unit, inverse, gain_ref[...])
    grad_mid_ref[...] = grad_mid
    branch_ref[...] = grad_mid.astype(BF16)


def turn(order, at, second_sums, mid_rows, out_grad, gain):
    return order.call(
        turn_kernel,
        "turn",
        (like(TOK, D), like(TOK, D, dtype=F32), like(1, D, dtype=F32)),
        (at, *second_sums, mid_rows, out_grad, gain[None, :]),
        in_specs=[SMEM] + [WHOLE] * 6,
        out_specs=(WHOLE,) * 3,
    )


def back_kernel(at_ref, b0, b1, b2a, b2b, b3, own_ref, other_ref, *refs):
    outs, rows_ref, weights = refs[:4], refs[4], refs[5]
    for block_ref, (d, first, count) in zip((b0, b1, b2a, b2b, b3), RING_ROWS):
        at = pl.ds(pl.multiple_of((at_ref[3] + d) % 4 * TOK + first, count), count)
        rows_ref[at, :] = block_ref[...]
    for d in range(4):
        head_weights(at_ref, own_ref, other_ref, weights, d)
    total = nt(weights[...], rows_ref[...]).astype(BF16)
    for d, out_ref in enumerate(outs):
        out_ref[...] = total[d * HEAD_V : (d + 1) * HEAD_V, :]


def back_projection(order, at, branch_blocks, weights):
    return order.call(
        back_kernel,
        "back_projection",
        (like(HEAD_V, GROUP),) * 4 + (like(GROUP, D),),
        (at, *branch_blocks, *weights),
        [pltpu.VMEM((GROUP, D), BF16)],
        in_specs=[SMEM] + [WHOLE] * 7,
        out_specs=(WHOLE,) * 5,
    )


def own_first(at_ref, out, block, rows):
    for own in (0, 1):
        for k in range(4):
            columns = pl.ds(piece_at(at_ref, k, own == 0), PIECE)
            piece = own * 4 + k
            out[rows, piece * PIECE : (piece + 1) * PIECE] = block[:, columns]


def out_grads_kernel(at_ref, m0, m1, m2, m3, branch_ref, out_ref, rows):
    own_first(at_ref, rows, branch_ref, slice(0, GROUP))
    for back, mixed_ref in enumerate((m0, m1, m2, m3)):
        out_ref[(4 - back) % 4] = nn(mixed_ref[...], rows[...]).astype(BF16)


def out_grads(order, at, mixed, branch_rows):
    return order.call(
        out_grads_kernel,
        "out_grads",
        like(4, HEAD_V, D),
        (at, *mixed, branch_rows),
        [pltpu.VMEM((GROUP, D), BF16)],
        in_specs=[SMEM] + [WHOLE] * 5,
        out_specs=WHOLE,
    )


BOTH_ROWS = HEAD_V + HEAD_ROWS + 16


def head_grads_kernel(at_ref, *refs):
    (g0, g1, g2, g3), weights, normed_ref, gain_ref = refs[:4], refs[4:9], refs[9], refs[10]
    out_grad_ref, second_ref, own_ref, other_ref, rows = refs[11:]
    own_first(at_ref, rows, normed_ref, slice(0, GROUP))
    rest = HEAD_ROWS - HALF_ROWS
    places = (
        (g0, ((weights[0], HEAD_ROWS),)),
        (g3, ((weights[1], HEAD_ROWS),)),
        (g2, ((weights[2], HALF_ROWS), (weights[3], rest))),
        (g1, ((weights[4], HEAD_ROWS),)),
    )
    for own in (0, 1):
        sent_ref = own_ref if own == 0 else other_ref
        for k in range(4):
            columns = pl.ds(piece_at(at_ref, k, own == 0), PIECE)
            piece = slice((own * 4 + k) * PIECE, (own * 4 + k + 1) * PIECE)
            gain_part = jnp.zeros((1, PIECE), F32)
            for d, (grads_ref, w_refs) in enumerate(places):
                part = nn(grads_ref[...], rows[:, piece])
                first = 0
                for w_ref, count in w_refs:
                    weighted = part[first : first + count] * w_ref[:count, columns].astype(F32)
                    gain_part = gain_part + jnp.sum(weighted, axis=0, keepdims=True)
                    first += count
                sent_ref[d, k, :HEAD_V] = out_grad_ref[d, :, piece]
                sent_ref[d, k, HEAD_V : HEAD_V + HEAD_ROWS] = part.astype(BF16)
            gain_part = gain_part / gain_ref[:, columns]
            gain_rows = jnp.where(
                lax.broadcasted_iota(jnp.int32, (16, PIECE), 0) == 0,
                gain_part,
                second_ref[:, columns],
            ).astype(BF16)
            for d in range(4):
                sent_ref[d, k, HEAD_V + HEAD_ROWS :] = gain_rows


def head_grads(order, at, grads, head_blocks, normed, gain, out_part, second_part, wait):
    both = like(4, 4, BOTH_ROWS, PIECE)
    return order.call(
        head_grads_kernel,
        "head_grads",
        (both, both),
        (at, *grads, *head_blocks, normed, gain[None, :], out_part, second_part),
        [pltpu.VMEM((GROUP, D), BF16)],
        wait,
        in_specs=[SMEM] + [WHOLE] * 13,
        out_specs=(WHOLE,) * 2,
    )


def add_kernel(at_ref, mine_ref, other_ref, *outs):
    for d, out_ref in enumerate(outs):
        out_ref[...] = (mine_ref[d].astype(F32) + other_ref[d].astype(F32)).astype(BF16)


def add_blocks(order, at, mine, other):
    return order.call(
        add_kernel,
        "add_blocks",
        (like(4, BOTH_ROWS, PIECE),) * 4,
        (at, mine, other),
        in_specs=[SMEM] + [WHOLE] * 2,
        out_specs=(WHOLE,) * 4,
    )


def first_kernel(at_ref, *refs):
    grads, (w0, w1, w2a, w2b, w3), outs = refs[:4], refs[4:9], refs[9:14]
    rest = HEAD_ROWS - HALF_ROWS
    for d in range(4):
        columns = at_place(at_ref, d)
        part = tn(grads[0][:, columns], w0[:HEAD_ROWS, :])
        part = part + tn(grads[3][:, columns], w1[:HEAD_ROWS, :])
        part = part + tn(grads[1][:, columns], w3[:HEAD_ROWS, :])
        part = part + tn(grads[2][:HALF_ROWS, columns], w2a[...])
        part = (part + tn(grads[2][HALF_ROWS:, columns], w2b[:rest, :])).astype(BF16)
        for out_ref, (place, first, count) in zip(outs, RING_ROWS):
            if place == d:
                out_ref[...] = part[first : first + count]


def first_part(order, at, grads, head_blocks, wait):
    return order.call(
        first_kernel,
        "first_part",
        RING_LIKE,
        (at, *grads, *head_blocks),
        wait=wait,
        in_specs=[SMEM] + [WHOLE] * 9,
        out_specs=(WHOLE,) * 5,
    )


def collect_kernel(turned, at_ref, *refs):
    outs = refs[5:]
    for own in (True, False):
        for d in range(4):
            columns = pl.ds(piece_at(at_ref, d, own), PIECE)
            first = 0
            for i, out_ref in enumerate(outs):
                rows = out_ref.shape[1 if i == turned else 0]
                at = slice(first, first - (-rows // 16 * 16))
                block = (refs[d][at, :] if own else refs[4][d, at, :]).astype(F32)[:rows]
                if i == turned:
                    out_ref[columns, :] = jnp.transpose(block)
                else:
                    out_ref[:, columns] = block
                first += -rows // 16 * -16


def collect(order, at, mine, name, *rows, turned=None):
    other = swapped(jnp.stack(mine))
    return order.call(
        lambda *refs: collect_kernel(turned, *refs),
        name,
        tuple(
            like(D, r, dtype=F32) if i == turned else like(r, D, dtype=F32)
            for i, r in enumerate(rows)
        ),
        (at, *mine, other),
        in_specs=[SMEM] + [WHOLE] * 5,
        out_specs=(WHOLE,) * len(rows),
    )


def after(array, *needed):
    return lax.optimization_barrier((array, *needed))[0]


def body(
    tokens,
    doc_start,
    gain_first,
    w_query,
    w_key,
    w_value,
    w_out,
    gain_second,
    w_gate,
    w_up,
    w_down,
    out_grad,
):
    order = Order()
    at = jnp.stack([lax.axis_index(a) for a in AXES]).astype(jnp.int32)
    x_at, core, z_at, y_at = (at[i] for i in range(4))

    token_blocks = ring_gathered(tokens, "y")
    out_half = lax.dynamic_slice_in_dim(w_out, core * (HEAD_V // 2), HEAD_V // 2, 0)
    w_head = jnp.concatenate([w_query.T, w_key.T, w_value.T, out_half], axis=0)
    head_blocks = ring_gathered(w_head, "z")
    feed_half = jnp.concatenate([w_gate.T, w_up.T, w_down], axis=0)
    feed_half = lax.dynamic_slice_in_dim(feed_half, core * 1024, 1024, 1)
    *qkv, group_normed = project(order, at, token_blocks, head_blocks, gain_first, ())
    feed_half = after(feed_half, *token_blocks[2:4], *head_blocks[2:4])
    feed_mine = lax.all_gather(feed_half, "z", axis=0)
    qkv = exchanged(qkv, "z")
    out_mine = jnp.stack([block[-(HEAD_V // 2) :] for block in (*head_blocks[:2], *head_blocks[3:])])
    out_mine = after(out_mine, *qkv)
    out_weights = (out_mine, swapped(out_mine))
    cot_rows = jnp.broadcast_to(after(out_grad, group_normed)[None], (4, TOK, D))
    cot_rows = lax.all_to_all(cot_rows, "y", 0, 0)

    positions = jnp.arange(SEQ, dtype=jnp.int32)
    start_row = lax.cummax(jnp.where(doc_start != 0, positions, 0))[None, :]
    *mixed, numer, denom, qkv = attention_forward(order, at, qkv, start_row, ())
    mixed = exchanged(mixed, "z")
    p0, p1, *p2, p3 = out_projection(order, at, mixed, out_weights, (cot_rows,))
    parts = (p0, *ring_end(ring_start(p2, "y"), p1, p3, "y"))
    mid_rows, second_normed = middle(order, at, parts, tokens, gain_second, ())

    cot_blocks = [out_grad] + [
        lax.dynamic_slice(cot_rows, ((y_at + d) % 4, first, 0), (1, count, D))[0]
        for d, first, count in RING_ROWS[1:]
    ]
    second_blocks = ring_gathered(second_normed, "y")
    feed_mine = after(feed_mine, second_blocks[1], second_blocks[4])
    feed_weights = (feed_mine, swapped(feed_mine))
    hidden, gate_delta, up_delta, s0, s1, *s2, s3 = feed(
        order, at, second_blocks, cot_blocks, feed_weights
    )
    arrived = ring_start(s2, "y")
    second_sums = (s0, *ring_end(arrived, s1, s3, "y"))
    deltas = (gate_delta, up_delta)
    (gu_grads,) = feed_grads(order, at, deltas, second_blocks, False, wait=arrived)
    gu_grads = swapped(gu_grads)
    (down_grads,) = feed_grads(order, at, (hidden,), cot_blocks, True)
    down_grads = swapped(down_grads)

    grad_branch, grad_mid, gain_second_part = turn(
        order, at, second_sums, mid_rows, out_grad, gain_second
    )
    branch_blocks = ring_gathered(grad_branch, "y")
    (gu_grads,) = feed_grads(
        order,
        at,
        deltas,
        second_blocks,
        False,
        (gu_grads,),
        wait=(branch_blocks[1], branch_blocks[4]),
    )
    gu_sum = lax.psum_scatter(
        gu_grads.reshape(16, 2 * HID, PIECE), ("x", "z"), scatter_dimension=0
    )
    b_parts = down(order, at, hidden, feed_weights, ())
    *grad_mixed, branch_rows = back_projection(order, at, branch_blocks, out_weights)
    grad_mixed = exchanged(grad_mixed, "z")
    b_parts = lax.all_to_all(after(b_parts, branch_rows), "y", 0, 0)
    (down_grads,) = feed_grads(order, at, (hidden,), cot_blocks, True, (down_grads,))
    out_part = out_grads(order, at, mixed, branch_rows)
    grads = attention_backward(order, at, qkv, grad_mixed, numer, denom, start_row, ())
    grads = exchanged(grads, "z")

    def added(blocks):
        total = (blocks[0].astype(F32) + blocks[1].astype(F32)) + (
            blocks[2].astype(F32) + blocks[3].astype(F32)
        )
        return total.astype(BF16)

    mine, other = head_grads(
        order,
        at,
        grads,
        head_blocks,
        group_normed,
        gain_first,
        out_part,
        gain_second_part,
        (b_parts,),
    )
    down_grads = lax.all_to_all(after(down_grads, b_parts), "x", 0, 0)
    other = swapped(other)
    f0, f1, *f2, f3 = first_part(order, at, grads, head_blocks, ())
    head_part = added(exchanged(add_blocks(order, at, mine, other), "z"))
    f_arrived = ring_start(f2, "y")
    head_part = after(head_part, *f_arrived)
    from_back, from_ahead = ring_end(f_arrived, f1, f3, "y")
    gu_blocks = gathered(gu_sum, "x")
    head_part = after(head_part, *gu_blocks[1:])
    head_sum = added(exchanged([head_part[d] for d in range(4)], "x"))
    down_grads = after(down_grads, *gu_blocks[1:])
    down_part = jnp.sum(down_grads.astype(F32), axis=0).astype(BF16)
    down_sum = added(exchanged([down_part[d] for d in range(4)], "z"))
    grad_first = f0.astype(F32) + from_back.astype(F32) + from_ahead.astype(F32)
    block_out = mid_rows + jnp.sum(b_parts.astype(F32), axis=0)
    x_rows = tokens.astype(F32)
    first_inv = inverse_rms(x_rows)
    input_grad = grad_mid + norm_back(grad_first, x_rows * first_inv, first_inv, gain_first)

    grad_gate, grad_up = collect(order, at, gu_blocks, "collect_gate_up", HID, HID)
    rest_sum = jnp.concatenate([head_sum, down_sum], axis=0)
    rest_sum = after(rest_sum, from_back, from_ahead)
    rest_blocks = gathered(rest_sum, "x")
    rest_blocks = lax.optimization_barrier((*rest_blocks, grad_gate))[:4]
    grad_out, grad_query, grad_key, grad_value, gains, grad_down = collect(
        order,
        at,
        list(rest_blocks),
        "collect_rest",
        HEAD_V,
        FEAT,
        FEAT,
        HEAD_V,
        2,
        HID,
        turned=3,
    )
    gains = gathered(gains, "y")
    gains = (gains[0] + gains[1]) + (gains[2] + gains[3])
    return (
        block_out,
        input_grad,
        gains[0],
        grad_query.T,
        grad_key.T,
        grad_value,
        grad_out,
        gains[1],
        grad_gate.T,
        grad_up.T,
        grad_down,
    )


def solution(mesh):
    fine = Mesh(mesh.devices.reshape(4, 2, 4, 4), AXES)
    rows, dp, mp = P(AXES, None), P(("x", "core")), ("z", "y")
    return jax.shard_map(
        body,
        mesh=fine,
        in_specs=(
            rows,
            dp,
            P(),
            P(None, mp),
            P(None, mp),
            P(None, mp),
            P(mp, None),
            P(),
            P(None, mp),
            P(None, mp),
            P(mp, None),
            rows,
        ),
        out_specs=(
            rows,
            rows,
            P(),
            P(None, mp),
            P(None, mp),
            P(None, mp),
            P(mp, None),
            P(),
            P(None, mp),
            P(None, mp),
            P(mp, None),
        ),
        check_vma=False,
    )
```
